128 devices in a mesh: tm: 32 (over x, z, core), chan: 4 (over y).
Axes of the slice: x: 4, y: 4, z: 4, core: 2. Of those that a mesh axis runs over, the one named last changes fastest.
Arguments:
- raw: bfloat16 [12288, 16384], P(('tm', 'chan')), may hold values from -6 to 6
- taps: bfloat16 [127], replicated, may hold values from -0.5 to 0.5
- row_channel: int32 [12288], replicated, may hold values from 0 to 12287, each once
- ref_channel: int32 [256], replicated, may hold values from 0 to 12287, as said below
- owner_of_row: int32 [12288, 1], P(('tm', 'chan')), may hold values from 0 to 127; in each aligned block of 96 rows (0 to 95, 96 to 191, ...) at most 2 rows name the same one
Outputs:
- tiles: float32 [128, 256, 4096], P(('tm', 'chan'))
The draws below stay inside these ranges and needn't reach their ends.
Inputs may be any that keep to these rules, and one draw needn't show every extreme that they name: `ref_channel`: distinct channel ids. `owner_of_row`: within each aligned block of 96 rows, at most 2 rows name the same setup.
All inputs are finite; a program needn't handle non-finite values.
Results may differ from the reference program's by a relative error of at most 0.013.
Values may be sent and summed in bfloat16 or wider, within the bound.
No kernel may reach another device: no remote copies, remote signals or barrier semaphores. Data moves between devices by JAX's collectives and lax.ppermute only.
A program may use at most 192 MiB of HBM per device.

```python
import math
import jax
import jax.numpy as jnp
import numpy as np
from jax import lax

C = 12288
NREF = 256
LAGS = 16
TAPS = 127
STRIDE = 8
SAMPLES = 16384
NDEC = 2048
ROWS_DEV = 96
CAP = 2
N_TM = 32
DEVICES = 128


def draw_ref_channel(key, part):
    key = jax.random.fold_in(key, 11)
    return jax.random.permutation(key, C)[:NREF].astype(jnp.int32)


def level_of(key, shape, cuts, smallest, high):
    factor_of = 1.0
    for dim, shards_of in cuts:
        heights = jax.random.uniform(jax.random.fold_in(jax.random.fold_in(key, 6), dim), (shards_of,), jnp.float32, smallest / len(cuts), high / len(cuts))
        factor_of = factor_of * jnp.repeat(jnp.exp(heights), shape[dim] // shards_of).reshape((-1,) + (1,) * (len(shape) - 1 - dim))
    return factor_of


def routed_block(stream_key, own, number, rows, count, top, limit, lean):
    order = jax.random.permutation(stream_key, count)
    crowded, common = portions_of(count, rows * top, limit, lean, True), portions_of(count, rows * top, limit, lean, False)
    places = jnp.arange(count)

    def named(tallies, turn):
        used = int((tallies > 0).sum())
        fixed = max(1, used // 4)
        moved = fixed + (places - fixed + turn * (used - fixed)) % max(1, count - fixed)
        return jnp.zeros((count,), jnp.int32).at[order[jnp.where(places < fixed, places, moved)]].set(jnp.asarray(tallies, jnp.int32))

    tallies = jnp.where(number % 4 == 0, named(crowded, number // 4), named(common, number - number // 4 - 1))
    mixed = jax.random.permutation(jax.random.fold_in(own, 3), count)
    source_of, sink = mixed[0:count // 2 * 2:2], mixed[1:count // 2 * 2:2]
    room = jnp.minimum(tallies[source_of] - 1, limit - tallies[sink]) // 2
    room = jnp.where((source_of == order[0]) | (sink == order[0]) | (tallies[sink] == 0), 0, jnp.maximum(room, 0))
    moved = jax.random.randint(jax.random.fold_in(own, 4), (count // 2,), 0, 1 << 20) % (room + 1)
    tallies = tallies.at[source_of].add(-moved).at[sink].add(moved)
    labels = jnp.searchsorted(jnp.cumsum(tallies), jnp.arange(rows * top), side="right").astype(jnp.int32)
    table = labels.reshape(top, rows).T
    table = table[jax.random.permutation(jax.random.fold_in(own, 1), rows)]
    turn = jax.random.randint(jax.random.fold_in(own, 2), (rows, 1), 0, top)
    return jnp.take_along_axis(table, (jnp.arange(top)[None, :] + turn) % top, axis=1)


def portions_of(count, total, limit, slope, full):
    weights = [(1 << 20) // math.isqrt(grade ** slope) + 1 for grade in range(1, count + 1)]
    largest = limit if full else min(limit, max(-(-total // count), total * weights[0] // sum(weights)))
    least = 1 if total - largest >= count - 1 else 0
    given, spare = [largest] + [least] * (count - 1), total - largest - least * (count - 1)
    while spare > 0:
        free = [i for i in range(1, count) if given[i] < largest] or [i for i in range(1, count) if given[i] < limit]
        whole, budget = sum([weights[i] for i in free]), spare
        for i in free:
            addition = min(limit - given[i], max(1, budget * weights[i] // whole), spare)
            given[i] = given[i] + addition
            spare = spare - addition
    return np.array(given)


def centred(own_key, shape, spread, limit, cuts=(), kind=jnp.bfloat16):
    level = level_of(own_key, shape, cuts, -0.22, 0.18) if cuts else 1.0
    result = jax.random.normal(own_key, shape, jnp.float32) * spread * level
    return jnp.minimum(jnp.maximum(result, -limit), limit).astype(kind)


def setup_inputs(seed: int = 0) -> dict:
    key_list = jax.random.split(jax.random.key(seed), 6)
    raw = centred(key_list[0], (C, SAMPLES), 1.0, 6.0, ((0, 128),))
    taps = centred(key_list[1], (TAPS,), TAPS ** -0.5, 0.5)
    row_channel = jax.random.permutation(key_list[2], C).astype(jnp.int32)
    ref_channel = draw_ref_channel(jax.random.fold_in(key_list[5], 71), 0)
    owner_of_row_keys = jax.random.split(jax.random.fold_in(key_list[4], 1), C // ROWS_DEV)
    owner_of_row_turns = jax.random.permutation(jax.random.fold_in(key_list[4], 3), C // ROWS_DEV)
    owner_of_row = jax.vmap(lambda own, number: routed_block(jax.random.fold_in(key_list[4], 2), own, number, ROWS_DEV, DEVICES, 1, CAP, 2))(owner_of_row_keys, owner_of_row_turns).reshape((C, 1))
    return dict(raw=raw, taps=taps, row_channel=row_channel, ref_channel=ref_channel, owner_of_row=owner_of_row)


def reference(raw, taps, row_channel, ref_channel, owner_of_row):
    total = NDEC
    nq = (TAPS + STRIDE - 1) // STRIDE
    half = TAPS // 2
    table = jnp.pad(taps.astype(jnp.float32), (0, nq * STRIDE - TAPS)).reshape(nq, STRIDE)
    block_rows = math.gcd(C, 256)
    dslab = total // N_TM

    def decimate(block):
        padded = jnp.pad(block.astype(jnp.float32), ((0, 0), (half, nq * STRIDE - half)))
        pieces = padded.reshape(block_rows, total + nq, STRIDE)
        accum = jnp.zeros((block_rows, total), jnp.float32)
        for q in range(nq):
            accum = accum + jnp.einsum('rnm,m->rn', pieces[:, q:q + total], table[q], precision=lax.Precision.HIGHEST)
        return accum.astype(jnp.bfloat16)
    decimated = lax.map(decimate, raw.reshape(C // block_rows, block_rows, SAMPLES)).reshape(C, total)
    inverse = jnp.zeros((C,), jnp.int32).at[row_channel].set(jnp.arange(C, dtype=jnp.int32))
    refs = decimated[inverse[ref_channel]].astype(jnp.float32).reshape(NREF, N_TM, dslab)
    extended = jnp.concatenate([decimated, jnp.zeros((C, LAGS), jnp.bfloat16)], axis=1)

    def correlate(block):
        outputs = []
        for lag in range(1, LAGS + 1):
            shifted = block[:, lag:lag + total].astype(jnp.float32).reshape(block_rows, N_TM, dslab)
            part = jnp.einsum('btn,jtn->tbj', shifted, refs, precision=lax.Precision.HIGHEST)
            rounded = lax.optimization_barrier(part.astype(jnp.bfloat16))
            outputs.append(lax.optimization_barrier(jnp.sum(rounded.astype(jnp.float32), axis=0)))
        return jnp.concatenate(outputs, axis=1)
    summed = lax.map(correlate, extended.reshape(C // block_rows, block_rows, total + LAGS))
    rows = summed.reshape(C, LAGS * NREF) * (1.0 / math.sqrt(NDEC))
    owner = owner_of_row[:, 0].reshape(DEVICES, ROWS_DEV)
    hits = (owner[:, :, None] == jnp.arange(DEVICES, dtype=jnp.int32)[None, None, :]).astype(jnp.int32)
    rank = lax.optimization_barrier(jnp.sum(hits * (jnp.cumsum(hits, axis=1) - 1), axis=2))
    source = jnp.broadcast_to(jnp.arange(DEVICES, dtype=jnp.int32)[:, None], (DEVICES, ROWS_DEV))
    slot = (source * CAP + rank).reshape(-1)
    tiles = jnp.zeros((DEVICES, DEVICES * CAP, LAGS * NREF), jnp.float32)
    return tiles.at[owner.reshape(-1), slot].set(rows)
```

```python
import math

import jax
import jax.numpy as jnp
from jax import lax
from jax.experimental import pallas as pl
from jax.experimental.pallas import tpu as pltpu
from jax.sharding import PartitionSpec as P

LAGS = 16
TAPS = 127
STRIDE = 8
NREF = 256
LANES = 128
BLOCK = 128
HALO = 128
AXES = ("tm", "chan")
NT = (((1,), (1,)), ((), ()))


def dot_nt(a, b):
    return lax.dot_general(a, b, NT, preferred_element_type=jnp.float32)


def decimate_kernel(raw_ref, taps_ref, ids_ref, refch_ref, owner_ref, rows_ref, refs_ref, line, dect, stage):
    rows, samples = raw_ref.shape
    devices = rows_ref.shape[0] // 32
    window = BLOCK * STRIDE + 2 * HALO
    line[...] = jnp.zeros_like(line)
    line[0:1, 0:TAPS] = taps_ref[...].astype(jnp.float32)
    band = pltpu.roll(
        jnp.broadcast_to(line[0:1, :], (BLOCK, window)),
        HALO - TAPS // 2,
        1,
        stride=STRIDE,
        stride_axis=0,
    ).astype(jnp.bfloat16)
    blocks = samples // (BLOCK * STRIDE)
    for m in range(blocks):
        lo, hi = m * BLOCK * STRIDE - HALO, (m + 1) * BLOCK * STRIDE + HALO
        first, last = max(lo, 0), min(hi, samples)
        part = dot_nt(band[:, first - lo : last - lo], raw_ref[:, first:last])
        dect[m * BLOCK : (m + 1) * BLOCK, :rows] = part.astype(jnp.bfloat16).astype(jnp.float32)
    owner = owner_ref[...]
    hits = lax.broadcasted_iota(jnp.int32, (devices, rows), 0) == owner
    before = (
        lax.broadcasted_iota(jnp.int32, (rows, rows), 0)
        < lax.broadcasted_iota(jnp.int32, (rows, rows), 1)
    ).astype(jnp.bfloat16)
    rank = jnp.dot(hits.astype(jnp.bfloat16), before, preferred_element_type=jnp.float32)
    one = hits.astype(jnp.float32)
    first_row = jnp.where(rank < 0.5, one, 0.0)
    second_row = one - first_row
    refcol = jnp.transpose(jnp.broadcast_to(refch_ref[...], (LANES, NREF)))[:, :rows]
    ref_rows = (refcol == ids_ref[...]).astype(jnp.float32)
    select = jnp.concatenate([first_row, second_row, ref_rows], axis=0).astype(jnp.bfloat16)
    for b in range(0, LAGS, 2):
        planes = jnp.concatenate(
            [dect[pl.ds(b + h, LANES, stride=LAGS), :][:, :rows] for h in range(2)], axis=0
        ).astype(jnp.bfloat16)
        picked = dot_nt(select, planes)
        for s in range(4):
            for h in range(2):
                stage[s // 2, pl.ds((s % 2) * LAGS + b + h, devices, stride=2 * LAGS), :] = picked[
                    s * devices : (s + 1) * devices, h * LANES : (h + 1) * LANES
                ]
    rows_ref[...] = stage[0].astype(jnp.bfloat16)
    refs_ref[...] = stage[1].astype(jnp.bfloat16)


def spread_kernel(got_ref, out_ref):
    size, width = got_ref.shape
    block = 2 * LAGS
    total = jnp.sum(got_ref[...].astype(jnp.float32).reshape(size // block, block, width), axis=0)
    out_ref[...] = (
        jnp.broadcast_to(total[None], (size // block, block, width))
        .reshape(size, width)
        .astype(jnp.bfloat16)
    )


def correlate_kernel(rows_ref, refs_ref, out_ref, wide, ext, ref_planes):
    step = pl.program_id(0)
    devices = rows_ref.shape[0] // 32
    total = LAGS * LANES

    @pl.when(step == 0)
    def _():
        wide[...] = refs_ref[...].astype(jnp.float32)
        for s in range(2):
            for b in range(LAGS):
                ref_planes[s * devices : (s + 1) * devices, b * LANES : (b + 1) * LANES] = wide[
                    pl.ds(s * LAGS + b, devices, stride=2 * LAGS), :
                ].astype(jnp.bfloat16)
        wide[...] = rows_ref[...].astype(jnp.float32)
        last_lane = lax.broadcasted_iota(jnp.int32, (2 * devices, LANES), 1) == LANES - 1
        for b in range(LAGS):
            plane = wide[pl.ds(b, 2 * devices, stride=LAGS), :]
            ext[:, b * LANES : (b + 1) * LANES] = plane.astype(jnp.bfloat16)
            moved = jnp.where(last_lane, 0.0, pltpu.roll(plane, LANES - 1, 1))
            ext[:, total + b * LANES : total + (b + 1) * LANES] = moved.astype(jnp.bfloat16)

    start = pl.multiple_of((step + 1) * LANES, LANES)
    out_ref[0] = dot_nt(ext[:, pl.ds(start, total)], ref_planes[...]) * (1.0 / math.sqrt(total))


def on_device(raw, taps, row_channel, ref_channel, owner_of_row):
    devices = lax.axis_size("tm") * lax.axis_size("chan")
    rows_dev, samples = raw.shape
    total = samples // STRIDE
    own = lax.axis_index("tm") * lax.axis_size("chan") + lax.axis_index("chan")
    ids = lax.dynamic_slice_in_dim(row_channel, own * rows_dev, rows_dev).reshape(1, rows_dev)
    packet = jax.ShapeDtypeStruct((devices * 32, LANES), jnp.bfloat16)
    vmem = pl.BlockSpec(memory_space=pltpu.VMEM)
    rows_out, refs_out = pl.pallas_call(
        decimate_kernel,
        out_shape=(packet, packet),
        in_specs=[vmem] * 5,
        out_specs=(vmem, vmem),
        scratch_shapes=[
            pltpu.VMEM((8, BLOCK * STRIDE + 2 * HALO), jnp.float32),
            pltpu.VMEM((total, LANES), jnp.float32),
            pltpu.VMEM((2, devices * 32, LANES), jnp.float32),
        ],
        compiler_params=pltpu.CompilerParams(vmem_limit_bytes=40 << 20),
        name="decimate",
    )(raw, taps.reshape(1, TAPS), ids, ref_channel.reshape(1, NREF), owner_of_row.reshape(1, rows_dev))
    refs_in = lax.all_to_all(refs_out, AXES, 0, 0, tiled=True)
    rows_in = lax.all_to_all(rows_out, AXES, 0, 0, tiled=True)
    refs_mine = pl.pallas_call(
        spread_kernel,
        out_shape=packet,
        in_specs=[vmem],
        out_specs=vmem,
        compiler_params=pltpu.CompilerParams(vmem_limit_bytes=32 << 20),
        name="spread",
    )(refs_in)
    refs_all = lax.all_to_all(refs_mine, AXES, 0, 0, tiled=True)
    return pl.pallas_call(
        correlate_kernel,
        grid=(LAGS,),
        out_shape=jax.ShapeDtypeStruct((1, 2 * devices, LAGS * NREF), jnp.float32),
        in_specs=[vmem, vmem],
        out_specs=pl.BlockSpec((1, 2 * devices, NREF), lambda i: (0, 0, i)),
        scratch_shapes=[
            pltpu.VMEM((devices * 32, LANES), jnp.float32),
            pltpu.VMEM((2 * devices, 2 * total), jnp.bfloat16),
            pltpu.VMEM((NREF, total), jnp.bfloat16),
        ],
        compiler_params=pltpu.CompilerParams(vmem_limit_bytes=40 << 20),
        name="correlate",
    )(rows_in, refs_all)


def solution(mesh):
    in_specs = (P(AXES, None), P(), P(), P(), P(AXES, None))
    out_specs = P(AXES, None, None)
    return jax.shard_map(
        on_device, mesh=mesh, in_specs=in_specs, out_specs=out_specs, check_vma=False
    )
```

```python
import math

import jax
import jax.numpy as jnp
from jax import lax
from jax.experimental import pallas as pl
from jax.experimental.pallas import tpu as pltpu
from jax.sharding import Mesh
from jax.sharding import PartitionSpec as P

LAGS = 16
TAPS = 127
STRIDE = 8
NREF = 256
LANES = 128
BLOCK = 128
HALO = 128
CHIPS = 64
AXES = ("x", "z", "core", "chan")
SAME = ("x", "z", "chan")
NT = (((1,), (1,)), ((), ()))
VMEM = pl.BlockSpec(memory_space=pltpu.VMEM)
HBM = pl.BlockSpec(memory_space=pltpu.HBM)
F32, BF16 = jnp.float32, jnp.bfloat16


def dot_nt(a, b):
    return lax.dot_general(a, b, NT, preferred_element_type=F32)


def params(mib=48):
    return pltpu.CompilerParams(vmem_limit_bytes=mib << 20)


def iota(shape, dim):
    return lax.broadcasted_iota(jnp.int32, shape, dim)


def decimate_kernel(raw_hbm, taps_hbm, ids_hbm, refch_hbm, planes_ref, keep_ref, give_ref,
                    raw, taps, ids, refch, line, dect, stage, raw_sem, small_sem):
    rows, samples = raw.shape
    blocks = samples // (BLOCK * STRIDE)
    chunk = BLOCK * STRIDE
    loads = [
        pltpu.make_async_copy(
            raw_hbm.at[:, pl.ds(m * chunk, chunk)], raw.at[:, pl.ds(m * chunk, chunk)], raw_sem.at[m]
        )
        for m in range(blocks)
    ]
    small = [
        pltpu.make_async_copy(taps_hbm, taps, small_sem.at[0]),
        pltpu.make_async_copy(ids_hbm, ids, small_sem.at[1]),
        pltpu.make_async_copy(refch_hbm, refch, small_sem.at[2]),
    ]
    for copy in small + loads:
        copy.start()
    core = lax.axis_index("core")
    own = lax.axis_index(AXES)
    window = chunk + 2 * HALO
    small[0].wait()
    line[...] = jnp.zeros_like(line)
    line[0:1, 0:TAPS] = taps[...].astype(F32)
    band = pltpu.roll(
        jnp.broadcast_to(line[0:1, :], (BLOCK, window)), HALO - TAPS // 2, 1, stride=STRIDE, stride_axis=0
    ).astype(BF16)
    small[1].wait()
    small[2].wait()
    at = own * rows
    line0 = at // LANES
    line1 = jnp.minimum(line0 + 1, ids.shape[0] - 1)
    shift = at - line0 * LANES
    turn = LANES - shift
    pair = [
        pltpu.roll(jnp.broadcast_to(ids[pl.ds(i, 1), :], (8, LANES)), turn, 1) for i in (line0, line1)
    ]
    mine = jnp.where(iota((8, LANES), 1) < turn, pair[0], pair[1])[0:1, :rows]
    refcol = jnp.transpose(jnp.broadcast_to(refch[...], (LANES, NREF)))[:, :rows]
    select = jnp.where(refcol == mine, 1.0, 0.0).astype(BF16)
    for m in range(blocks):
        lo, hi = m * chunk - HALO, (m + 1) * chunk + HALO
        first, last = max(lo, 0), min(hi, samples)
        if m == 0:
            loads[0].wait()
        if m + 1 < blocks:
            loads[m + 1].wait()
        part = dot_nt(band[:, first - lo : last - lo], raw[:, first:last])
        dect[m * BLOCK : (m + 1) * BLOCK, :rows] = part.astype(BF16).astype(F32)
    for b in range(0, LAGS, 2):
        planes = jnp.concatenate(
            [dect[pl.ds(b + h, LANES, stride=LAGS), :] for h in range(2)], axis=0
        ).astype(BF16)
        planes_ref[b * LANES : (b + 2) * LANES, :] = planes
        picked = dot_nt(select, planes[:, :rows])
        for g in range(4):
            for h in range(2):
                stage[g // 2, pl.ds((g % 2) * LAGS + b + h, CHIPS, stride=2 * LAGS), :] = picked[
                    g * CHIPS : (g + 1) * CHIPS, h * LANES : (h + 1) * LANES
                ]
    shape = (CHIPS, 2 * LAGS, LANES)
    keep_ref[...] = stage[core].astype(BF16).reshape(shape)
    give_ref[...] = stage[1 - core].astype(BF16).reshape(shape)


def route_kernel(planes_ref, owner_ref, keep_ref, got_ref, packet_ref, stage):
    rows = owner_ref.shape[1]
    owner = owner_ref[...]
    chip = iota((CHIPS, rows), 0)
    before = (iota((rows, rows), 0) < iota((rows, rows), 1)).astype(BF16)
    parts = []
    for core in range(2):
        device = (chip // 4) * 8 + core * 4 + chip % 4
        one = jnp.where(device == owner, 1.0, 0.0)
        rank = jnp.dot(one.astype(BF16), before, preferred_element_type=F32)
        first = jnp.where(rank < 0.5, one, 0.0)
        parts += [first, one - first]
    select = jnp.concatenate(parts, axis=0).astype(BF16)
    for b in range(0, LAGS, 2):
        picked = dot_nt(select, planes_ref[b * LANES : (b + 2) * LANES, :][:, :rows])
        for g in range(4):
            for h in range(2):
                stage[pl.ds(g * LAGS + b + h, CHIPS, stride=4 * LAGS), :] = picked[
                    g * CHIPS : (g + 1) * CHIPS, h * LANES : (h + 1) * LANES
                ]
    packet_ref[:, : 4 * LAGS, :] = stage[...].astype(BF16).reshape(CHIPS, 4 * LAGS, LANES)
    packet_ref[:, 4 * LAGS :, :] = (keep_ref[...].astype(F32) + got_ref[...].astype(F32)).astype(BF16)


def spread_kernel(arrived_ref, spread_ref, give_ref):
    core = lax.axis_index("core")
    total = jnp.sum(arrived_ref[:, 4 * LAGS :, :].astype(F32), axis=0, keepdims=True)
    spread_ref[...] = jnp.broadcast_to(total, spread_ref.shape).astype(BF16)
    other = pl.multiple_of((1 - core) * 2 * LAGS, 2 * LAGS)
    give_ref[...] = arrived_ref[:, pl.ds(other, 2 * LAGS), :]


def widen_kernel(arrived_ref, got_ref, ext_ref, wide):
    core = lax.axis_index("core")
    size = CHIPS * 2 * LAGS
    mine = pl.multiple_of(core * 2 * LAGS, 2 * LAGS)
    wide[core] = arrived_ref[:, pl.ds(mine, 2 * LAGS), :].astype(F32).reshape(size, LANES)
    wide[1 - core] = got_ref[...].astype(F32).reshape(size, LANES)
    total = LAGS * LANES
    last_lane = iota((4 * CHIPS, LANES), 1) == LANES - 1
    for b in range(LAGS):
        halves = [wide[c, pl.ds(b, 2 * CHIPS, stride=LAGS), :].reshape(CHIPS // 4, 1, 8, LANES) for c in range(2)]
        plane = jnp.concatenate(halves, axis=1).reshape(4 * CHIPS, LANES)
        ext_ref[:, b * LANES : (b + 1) * LANES] = plane.astype(BF16)
        moved = jnp.where(last_lane, 0.0, pltpu.roll(plane, LANES - 1, 1))
        ext_ref[:, total + b * LANES : total + (b + 1) * LANES] = moved.astype(BF16)


def correlate_kernel(per, ext_ref, own_ref, other_ref, out_ref, wide, ref_planes):
    step = pl.program_id(0)
    total = LAGS * LANES
    size = CHIPS * 2 * LAGS

    @pl.when(step == 0)
    def _():
        core = lax.axis_index("core")
        wide[core] = own_ref[...].astype(F32).reshape(size, LANES)
        wide[1 - core] = other_ref[...].astype(F32).reshape(size, LANES)
        for g in range(4):
            for b in range(LAGS):
                ref_planes[g * CHIPS : (g + 1) * CHIPS, b * LANES : (b + 1) * LANES] = wide[
                    g // 2, pl.ds((g % 2) * LAGS + b, CHIPS, stride=2 * LAGS), :
                ].astype(BF16)

    start = pl.multiple_of((step * per + 1) * LANES, LANES)
    lagged = jnp.concatenate([ext_ref[:, pl.ds(start + i * LANES, total)] for i in range(per)], axis=0)
    sums = dot_nt(lagged, ref_planes[...]) * (1.0 / math.sqrt(total))
    for i in range(per):
        out_ref[0, :, i * NREF : (i + 1) * NREF] = sums[i * 4 * CHIPS : (i + 1) * 4 * CHIPS]


def swap_cores(x):
    return lax.ppermute(x, "core", [(0, 1), (1, 0)])


def on_device(raw, taps, row_channel, ref_channel, owner_of_row):
    rows_dev, samples = raw.shape
    total = samples // STRIDE
    window = BLOCK * STRIDE + 2 * HALO
    half = jax.ShapeDtypeStruct((CHIPS, 2 * LAGS, LANES), BF16)
    ids = row_channel.reshape(-1, LANES)
    planes, keep, give = pl.pallas_call(
        decimate_kernel,
        out_shape=(jax.ShapeDtypeStruct((total, LANES), BF16), half, half),
        in_specs=[HBM] * 4,
        out_specs=(VMEM, VMEM, VMEM),
        scratch_shapes=[
            pltpu.VMEM((rows_dev, samples), BF16),
            pltpu.VMEM((1, TAPS), BF16),
            pltpu.VMEM(ids.shape, jnp.int32),
            pltpu.VMEM((1, NREF), jnp.int32),
            pltpu.VMEM((8, window), F32),
            pltpu.VMEM((total, LANES), F32),
            pltpu.VMEM((2, CHIPS * 2 * LAGS, LANES), F32),
            pltpu.SemaphoreType.DMA((samples // (BLOCK * STRIDE),)),
            pltpu.SemaphoreType.DMA((3,)),
        ],
        compiler_params=params(60),
        name="decimate",
    )(raw, taps.reshape(1, TAPS), ids, ref_channel.reshape(1, NREF))
    got = swap_cores(give)
    packet = pl.pallas_call(
        route_kernel,
        out_shape=jax.ShapeDtypeStruct((CHIPS, 6 * LAGS, LANES), BF16),
        in_specs=[VMEM] * 4,
        out_specs=VMEM,
        scratch_shapes=[pltpu.VMEM((CHIPS * 4 * LAGS, LANES), F32)],
        compiler_params=params(),
        name="route",
    )(planes, owner_of_row.reshape(1, rows_dev), keep, got)
    arrived = lax.all_to_all(packet, SAME, 0, 0, tiled=True)
    spread, rows_give = pl.pallas_call(
        spread_kernel,
        out_shape=(half, half),
        in_specs=[VMEM],
        out_specs=(VMEM, VMEM),
        compiler_params=params(),
        name="spread",
    )(arrived)
    refs_own = lax.all_to_all(spread, SAME, 0, 0, tiled=True)
    rows_got = swap_cores(rows_give)
    ext = pl.pallas_call(
        widen_kernel,
        out_shape=jax.ShapeDtypeStruct((4 * CHIPS, 2 * total), BF16),
        in_specs=[VMEM, VMEM],
        out_specs=VMEM,
        scratch_shapes=[pltpu.VMEM((2, CHIPS * 2 * LAGS, LANES), F32)],
        compiler_params=params(),
        name="widen",
    )(arrived, rows_got)
    refs_other = swap_cores(refs_own)
    per = 4
    return pl.pallas_call(
        lambda *refs: correlate_kernel(per, *refs),
        grid=(LAGS // per,),
        out_shape=jax.ShapeDtypeStruct((1, 4 * CHIPS, LAGS * NREF), F32),
        in_specs=[VMEM, VMEM, VMEM],
        out_specs=pl.BlockSpec((1, 4 * CHIPS, per * NREF), lambda i: (0, 0, i)),
        scratch_shapes=[
            pltpu.VMEM((2, CHIPS * 2 * LAGS, LANES), F32),
            pltpu.VMEM((NREF, total), BF16),
        ],
        compiler_params=params(),
        name="correlate",
    )(ext, refs_own, refs_other)


def solution(mesh):
    parts = Mesh(mesh.devices.reshape(4, 4, 2, 4), AXES)
    return jax.shard_map(
        on_device,
        mesh=parts,
        in_specs=(P(AXES, None), P(), P(), P(), P(AXES, None)),
        out_specs=P(AXES, None, None),
        check_vma=False,
    )
```

```python
import math

import jax
import jax.numpy as jnp
from jax import lax
from jax.experimental import pallas as pl
from jax.experimental.pallas import tpu as pltpu
from jax.sharding import Mesh
from jax.sharding import PartitionSpec as P

LAGS = 16
TAPS = 127
STRIDE = 8
NREF = 256
LANES = 128
BLOCK = 128
HALO = 128
CHIPS = 64
AXES = ("x", "z", "core", "chan")
SAME = ("x", "z", "chan")
NT = (((1,), (1,)), ((), ()))
VMEM = pl.BlockSpec(memory_space=pltpu.VMEM)
HBM = pl.BlockSpec(memory_space=pltpu.HBM)
F32, BF16 = jnp.float32, jnp.bfloat16


def dot_nt(a, b):
    return lax.dot_general(a, b, NT, preferred_element_type=F32)


def params(mib=48):
    return pltpu.CompilerParams(vmem_limit_bytes=mib << 20)


def iota(shape, dim):
    return lax.broadcasted_iota(jnp.int32, shape, dim)


def decimate_kernel(raw_hbm, taps_hbm, ids_hbm, refch_hbm, dec_ref, keep_ref, give_ref,
                    raw, taps, ids, refch, line, dec, stage, raw_sem, small_sem):
    rows = dec_ref.shape[0]
    groups = raw_sem.shape[0]
    chunk = BLOCK * STRIDE
    window = chunk + 2 * HALO
    span = raw_hbm.shape[1] // groups
    loads = [
        pltpu.make_async_copy(
            raw_hbm.at[:, pl.ds(m * span, span)], raw.at[:, pl.ds(HALO + m * span, span)], raw_sem.at[m]
        )
        for m in range(groups)
    ]
    small = [
        pltpu.make_async_copy(taps_hbm, taps, small_sem.at[0]),
        pltpu.make_async_copy(ids_hbm, ids, small_sem.at[1]),
        pltpu.make_async_copy(refch_hbm, refch, small_sem.at[2]),
    ]
    for copy in small + loads:
        copy.start()
    core = lax.axis_index("core")
    own = lax.axis_index(AXES)
    raw[:, :HALO] = jnp.zeros((rows, HALO), BF16)
    raw[:, raw.shape[1] - HALO :] = jnp.zeros((rows, HALO), BF16)
    line[...] = jnp.zeros_like(line)
    small[0].wait()
    line[0:1, 0:TAPS] = taps[...].astype(F32)
    band = pltpu.roll(
        jnp.broadcast_to(line[0:1, :], (BLOCK, window)), HALO - TAPS // 2, 1, stride=STRIDE, stride_axis=0
    )
    band = jnp.transpose(band).astype(BF16)
    small[1].wait()
    small[2].wait()
    at = own * rows
    line0 = at // LANES
    line1 = jnp.minimum(line0 + 1, ids.shape[0] - 1)
    turn = LANES - (at - line0 * LANES)
    pair = [
        pltpu.roll(jnp.broadcast_to(ids[pl.ds(i, 1), :], (8, LANES)), turn, 1) for i in (line0, line1)
    ]
    mine = jnp.where(iota((8, LANES), 1) < turn, pair[0], pair[1])[0:1, :rows]
    refcol = jnp.transpose(jnp.broadcast_to(refch[...], (LANES, NREF)))[:, :rows]
    select = jnp.where(refcol == mine, 1.0, 0.0).astype(BF16)
    per = span // chunk
    loads[0].wait()
    for m in range(groups):
        if m + 1 < groups:
            loads[m + 1].wait()
        windows = [raw[:, pl.ds((m * per + i) * chunk, window)] for i in range(per)]
        part = jnp.dot(jnp.concatenate(windows, axis=0), band, preferred_element_type=F32).astype(BF16)
        for i in range(per):
            at = (m * per + i) * LANES
            dec[:, at : at + LANES] = part[i * rows : (i + 1) * rows].astype(F32)
    lane = iota((16, LANES), 1)
    for r in range(0, rows, 16):
        pieces = [dec[r : r + 16, m * LANES : (m + 1) * LANES] for m in range(LAGS)]
        for k in (1, 2, 4, 8):
            low = (lane & k) == 0
            for t in range(LAGS):
                if not t & k:
                    x, y = pieces[t], pieces[t | k]
                    pieces[t] = jnp.where(low, x, pltpu.roll(y, k, 1))
                    pieces[t | k] = jnp.where(low, pltpu.roll(x, LANES - k, 1), y)
        for b in range(LAGS):
            dec_ref[r : r + 16, b * LANES : (b + 1) * LANES] = pieces[b].astype(BF16)
    for b in range(0, LAGS, 2):
        picked = jnp.dot(select, dec_ref[:, b * LANES : (b + 2) * LANES], preferred_element_type=F32)
        for g in range(4):
            for h in range(2):
                stage[g // 2, pl.ds((g % 2) * LAGS + b + h, CHIPS, stride=2 * LAGS), :] = picked[
                    g * CHIPS : (g + 1) * CHIPS, h * LANES : (h + 1) * LANES
                ]
    shape = (CHIPS, 2 * LAGS, LANES)
    keep_ref[...] = stage[core].astype(BF16).reshape(shape)
    give_ref[...] = stage[1 - core].astype(BF16).reshape(shape)


def route_kernel(dec_ref, owner_ref, packet_ref, stage):
    rows = owner_ref.shape[1]
    owner = owner_ref[...]
    chip = iota((CHIPS, rows), 0)
    before = (iota((rows, rows), 0) < iota((rows, rows), 1)).astype(BF16)
    parts = []
    for core in range(2):
        device = (chip // 4) * 8 + core * 4 + chip % 4
        one = jnp.where(device == owner, 1.0, 0.0)
        rank = jnp.dot(one.astype(BF16), before, preferred_element_type=F32)
        first = jnp.where(rank < 0.5, one, 0.0)
        parts += [first, one - first]
    select = jnp.concatenate(parts, axis=0).astype(BF16)
    for b in range(0, LAGS, 2):
        picked = jnp.dot(select, dec_ref[:, b * LANES : (b + 2) * LANES], preferred_element_type=F32)
        for g in range(4):
            for h in range(2):
                stage[pl.ds(g * LAGS + b + h, CHIPS, stride=4 * LAGS), :] = picked[
                    g * CHIPS : (g + 1) * CHIPS, h * LANES : (h + 1) * LANES
                ]
    packet_ref[:, : 4 * LAGS, :] = stage[...].astype(BF16).reshape(CHIPS, 4 * LAGS, LANES)


def add_refs_kernel(packet_in, keep_ref, got_ref, packet_ref):
    del packet_in
    packet_ref[:, 4 * LAGS :, :] = (keep_ref[...].astype(F32) + got_ref[...].astype(F32)).astype(BF16)


def spread_kernel(arrived_ref, spread_ref, give_ref):
    core = lax.axis_index("core")
    total = jnp.sum(arrived_ref[:, 4 * LAGS :, :].astype(F32), axis=0, keepdims=True)
    spread_ref[...] = jnp.broadcast_to(total, spread_ref.shape).astype(BF16)
    other = pl.multiple_of((1 - core) * 2 * LAGS, 2 * LAGS)
    give_ref[...] = arrived_ref[:, pl.ds(other, 2 * LAGS), :]


def widen_kernel(arrived_ref, got_ref, ext_ref, wide):
    core = lax.axis_index("core")
    size = CHIPS * 2 * LAGS
    mine = pl.multiple_of(core * 2 * LAGS, 2 * LAGS)
    wide[core] = arrived_ref[:, pl.ds(mine, 2 * LAGS), :].astype(F32).reshape(size, LANES)
    wide[1 - core] = got_ref[...].astype(F32).reshape(size, LANES)
    total = LAGS * LANES
    lane = iota((4 * CHIPS, LANES), 1)
    for b in range(LAGS):
        halves = [wide[c, pl.ds(b, 2 * CHIPS, stride=LAGS), :].reshape(CHIPS // 4, 1, 8, LANES) for c in range(2)]
        plane = jnp.concatenate(halves, axis=1).reshape(4 * CHIPS, LANES)
        ext_ref[:, b * LANES : (b + 1) * LANES] = plane.astype(BF16)
        moved = jnp.where(
            lane < LANES - LAGS, pltpu.roll(plane, LANES - LAGS, 1), pltpu.roll(plane, LANES - LAGS - 1, 1)
        )
        moved = jnp.where(lane == LANES - 1, 0.0, moved)
        ext_ref[:, total + b * LANES : total + (b + 1) * LANES] = moved.astype(BF16)


def correlate_kernel(per, ext_ref, own_ref, other_ref, out_ref, wide, ref_planes):
    step = pl.program_id(0)
    total = LAGS * LANES
    size = CHIPS * 2 * LAGS

    @pl.when(step == 0)
    def _():
        core = lax.axis_index("core")
        wide[core] = own_ref[...].astype(F32).reshape(size, LANES)
        wide[1 - core] = other_ref[...].astype(F32).reshape(size, LANES)
        for g in range(4):
            for b in range(LAGS):
                ref_planes[g * CHIPS : (g + 1) * CHIPS, b * LANES : (b + 1) * LANES] = wide[
                    g // 2, pl.ds((g % 2) * LAGS + b, CHIPS, stride=2 * LAGS), :
                ].astype(BF16)

    start = pl.multiple_of((step * per + 1) * LANES, LANES)
    lagged = jnp.concatenate([ext_ref[:, pl.ds(start + i * LANES, total)] for i in range(per)], axis=0)
    sums = dot_nt(lagged, ref_planes[...]) * (1.0 / math.sqrt(total))
    for i in range(per):
        out_ref[0, :, i * NREF : (i + 1) * NREF] = sums[i * 4 * CHIPS : (i + 1) * 4 * CHIPS]


def swap_cores(x):
    return lax.ppermute(x, "core", [(0, 1), (1, 0)])


def on_device(raw, taps, row_channel, ref_channel, owner_of_row):
    rows_dev, samples = raw.shape
    total = samples // STRIDE
    window = BLOCK * STRIDE + 2 * HALO
    half = jax.ShapeDtypeStruct((CHIPS, 2 * LAGS, LANES), BF16)
    ids = row_channel.reshape(-1, LANES)
    dec, keep, give = pl.pallas_call(
        decimate_kernel,
        out_shape=(jax.ShapeDtypeStruct((rows_dev, total), BF16), half, half),
        in_specs=[HBM] * 4,
        out_specs=(VMEM, VMEM, VMEM),
        scratch_shapes=[
            pltpu.VMEM((rows_dev, samples + 2 * HALO), BF16),
            pltpu.VMEM((1, TAPS), BF16),
            pltpu.VMEM(ids.shape, jnp.int32),
            pltpu.VMEM((1, NREF), jnp.int32),
            pltpu.VMEM((8, window), F32),
            pltpu.VMEM((rows_dev, total), F32),
            pltpu.VMEM((2, CHIPS * 2 * LAGS, LANES), F32),
            pltpu.SemaphoreType.DMA((4,)),
            pltpu.SemaphoreType.DMA((3,)),
        ],
        compiler_params=params(54),
        name="decimate",
    )(raw, taps.reshape(1, TAPS), ids, ref_channel.reshape(1, NREF))
    got = swap_cores(give)
    packet_shape = jax.ShapeDtypeStruct((CHIPS, 6 * LAGS, LANES), BF16)
    packet = pl.pallas_call(
        route_kernel,
        out_shape=packet_shape,
        in_specs=[VMEM, VMEM],
        out_specs=VMEM,
        scratch_shapes=[pltpu.VMEM((CHIPS * 4 * LAGS, LANES), F32)],
        compiler_params=params(),
        cost_estimate=pl.CostEstimate(flops=100_000_000, bytes_accessed=4_000_000, transcendentals=0),
        name="route",
    )(dec, owner_of_row.reshape(1, rows_dev))
    packet = pl.pallas_call(
        add_refs_kernel,
        out_shape=packet_shape,
        in_specs=[VMEM] * 3,
        out_specs=VMEM,
        input_output_aliases={0: 0},
        compiler_params=params(),
        name="add_refs",
    )(packet, keep, got)
    arrived = lax.all_to_all(packet, SAME, 0, 0, tiled=True)
    spread, rows_give = pl.pallas_call(
        spread_kernel,
        out_shape=(half, half),
        in_specs=[VMEM],
        out_specs=(VMEM, VMEM),
        compiler_params=params(),
        name="spread",
    )(arrived)
    refs_own = lax.all_to_all(spread, SAME, 0, 0, tiled=True)
    rows_got = swap_cores(rows_give)
    ext = pl.pallas_call(
        widen_kernel,
        out_shape=jax.ShapeDtypeStruct((4 * CHIPS, 2 * total), BF16),
        in_specs=[VMEM, VMEM],
        out_specs=VMEM,
        scratch_shapes=[pltpu.VMEM((2, CHIPS * 2 * LAGS, LANES), F32)],
        compiler_params=params(),
        name="widen",
    )(arrived, rows_got)
    refs_other = swap_cores(refs_own)
    per = 4
    return pl.pallas_call(
        lambda *refs: correlate_kernel(per, *refs),
        grid=(LAGS // per,),
        out_shape=jax.ShapeDtypeStruct((1, 4 * CHIPS, LAGS * NREF), F32),
        in_specs=[VMEM, VMEM, VMEM],
        out_specs=pl.BlockSpec((1, 4 * CHIPS, per * NREF), lambda i: (0, 0, i)),
        scratch_shapes=[
            pltpu.VMEM((2, CHIPS * 2 * LAGS, LANES), F32),
            pltpu.VMEM((NREF, total), BF16),
        ],
        compiler_params=params(),
        name="correlate",
    )(ext, refs_own, refs_other)


def solution(mesh):
    parts = Mesh(mesh.devices.reshape(4, 4, 2, 4), AXES)
    return jax.shard_map(
        on_device,
        mesh=parts,
        in_specs=(P(AXES, None), P(), P(), P(), P(AXES, None)),
        out_specs=P(AXES, None, None),
        check_vma=False,
    )
```

```python
import math

import jax
import jax.numpy as jnp
from jax import lax
from jax.experimental import pallas as pl
from jax.experimental.pallas import tpu as pltpu
from jax.sharding import Mesh
from jax.sharding import PartitionSpec as P

LAGS = 16
TAPS = 127
STRIDE = 8
NREF = 256
LANES = 128
BLOCK = 128
HALO = 128
CHIPS = 64
AXES = ("x", "z", "core", "chan")
SAME = ("x", "z", "chan")
NT = (((1,), (1,)), ((), ()))
VMEM = pl.BlockSpec(memory_space=pltpu.VMEM)
HBM = pl.BlockSpec(memory_space=pltpu.HBM)
F32, BF16 = jnp.float32, jnp.bfloat16


def dot_nt(a, b):
    return lax.dot_general(a, b, NT, preferred_element_type=F32)


def params(mib=48):
    return pltpu.CompilerParams(vmem_limit_bytes=mib << 20)


def iota(shape, dim):
    return lax.broadcasted_iota(jnp.int32, shape, dim)


def decimate_kernel(raw_hbm, taps_hbm, ids_hbm, refch_hbm, dec_hbm, keep_hbm, give_hbm,
                    raw, taps, ids, refch, line, dec, planes, stage, keep, give, raw_sem, small_sem, out_sem):
    rows = planes.shape[0]
    groups = raw_sem.shape[0]
    chunk = BLOCK * STRIDE
    window = chunk + 2 * HALO
    span = raw_hbm.shape[1] // groups
    loads = [
        pltpu.make_async_copy(
            raw_hbm.at[:, pl.ds(m * span, span)], raw.at[:, pl.ds(HALO + m * span, span)], raw_sem.at[m]
        )
        for m in range(groups)
    ]
    small = [
        pltpu.make_async_copy(taps_hbm, taps, small_sem.at[0]),
        pltpu.make_async_copy(ids_hbm, ids, small_sem.at[1]),
        pltpu.make_async_copy(refch_hbm, refch, small_sem.at[2]),
    ]
    for copy in small + loads:
        copy.start()
    core = lax.axis_index("core")
    own = lax.axis_index(AXES)
    raw[:, :HALO] = jnp.zeros((rows, HALO), BF16)
    raw[:, raw.shape[1] - HALO :] = jnp.zeros((rows, HALO), BF16)
    line[...] = jnp.zeros_like(line)
    small[0].wait()
    line[0:1, 0:TAPS] = taps[...].astype(F32)
    band = pltpu.roll(
        jnp.broadcast_to(line[0:1, :], (BLOCK, window)), HALO - TAPS // 2, 1, stride=STRIDE, stride_axis=0
    )
    band = jnp.transpose(band).astype(BF16)
    small[1].wait()
    small[2].wait()
    at = own * rows
    line0 = at // LANES
    line1 = jnp.minimum(line0 + 1, ids.shape[0] - 1)
    turn = LANES - (at - line0 * LANES)
    pair = [
        pltpu.roll(jnp.broadcast_to(ids[pl.ds(i, 1), :], (8, LANES)), turn, 1) for i in (line0, line1)
    ]
    mine = jnp.where(iota((8, LANES), 1) < turn, pair[0], pair[1])[0:1, :rows]
    refcol = jnp.transpose(jnp.broadcast_to(refch[...], (LANES, NREF)))[:, :rows]
    select = jnp.where(refcol == mine, 1.0, 0.0).astype(BF16)
    per = span // chunk
    loads[0].wait()
    for m in range(groups):
        if m + 1 < groups:
            loads[m + 1].wait()
        windows = [raw[:, pl.ds((m * per + i) * chunk, window)] for i in range(per)]
        part = jnp.dot(jnp.concatenate(windows, axis=0), band, preferred_element_type=F32).astype(BF16)
        for i in range(per):
            at = (m * per + i) * LANES
            dec[:, at : at + LANES] = part[i * rows : (i + 1) * rows].astype(F32)
    lane = iota((16, LANES), 1)
    for r in range(0, rows, 16):
        pieces = [dec[r : r + 16, m * LANES : (m + 1) * LANES] for m in range(LAGS)]
        for k in (1, 2, 4, 8):
            low = (lane & k) == 0
            for t in range(LAGS):
                if not t & k:
                    x, y = pieces[t], pieces[t | k]
                    pieces[t] = jnp.where(low, x, pltpu.roll(y, k, 1))
                    pieces[t | k] = jnp.where(low, pltpu.roll(x, LANES - k, 1), y)
        for b in range(LAGS):
            planes[r : r + 16, b * LANES : (b + 1) * LANES] = pieces[b].astype(BF16)
    stores = [
        pltpu.make_async_copy(planes, dec_hbm, out_sem.at[0]),
        pltpu.make_async_copy(give, give_hbm, out_sem.at[1]),
        pltpu.make_async_copy(keep, keep_hbm, out_sem.at[2]),
    ]
    stores[0].start()
    for b in range(0, LAGS, 2):
        picked = jnp.dot(select, planes[:, b * LANES : (b + 2) * LANES], preferred_element_type=F32)
        for g in range(4):
            for h in range(2):
                stage[g // 2, pl.ds((g % 2) * LAGS + b + h, CHIPS, stride=2 * LAGS), :] = picked[
                    g * CHIPS : (g + 1) * CHIPS, h * LANES : (h + 1) * LANES
                ]
    shape = (CHIPS, 2 * LAGS, LANES)
    give[...] = stage[1 - core].astype(BF16).reshape(shape)
    stores[1].start()
    keep[...] = stage[core].astype(BF16).reshape(shape)
    stores[2].start()
    for store in stores:
        store.wait()


def route_kernel(dec_hbm, owner_ref, packet_ref, planes, stage, sem):
    load = pltpu.make_async_copy(dec_hbm, planes, sem)
    load.start()
    rows = owner_ref.shape[1]
    owner = owner_ref[...]
    chip = iota((CHIPS, rows), 0)
    before = (iota((rows, rows), 0) < iota((rows, rows), 1)).astype(BF16)
    parts = []
    for core in range(2):
        device = (chip // 4) * 8 + core * 4 + chip % 4
        one = jnp.where(device == owner, 1.0, 0.0)
        rank = jnp.dot(one.astype(BF16), before, preferred_element_type=F32)
        first = jnp.where(rank < 0.5, one, 0.0)
        parts += [first, one - first]
    select = jnp.concatenate(parts, axis=0).astype(BF16)
    load.wait()
    for b in range(0, LAGS, 2):
        picked = jnp.dot(select, planes[:, b * LANES : (b + 2) * LANES], preferred_element_type=F32)
        for g in range(4):
            for h in range(2):
                stage[pl.ds(g * LAGS + b + h, CHIPS, stride=4 * LAGS), :] = picked[
                    g * CHIPS : (g + 1) * CHIPS, h * LANES : (h + 1) * LANES
                ]
    packet_ref[:, : 4 * LAGS, :] = stage[...].astype(BF16).reshape(CHIPS, 4 * LAGS, LANES)


def add_refs_kernel(packet_in, keep_ref, got_ref, packet_ref):
    del packet_in
    packet_ref[:, 4 * LAGS :, :] = (keep_ref[...].astype(F32) + got_ref[...].astype(F32)).astype(BF16)


def spread_kernel(arrived_ref, spread_ref):
    total = jnp.sum(arrived_ref[:, 4 * LAGS :, :].astype(F32), axis=0, keepdims=True)
    spread_ref[...] = jnp.broadcast_to(total, spread_ref.shape).astype(BF16)


def give_kernel(arrived_ref, give_ref):
    other = pl.multiple_of((1 - lax.axis_index("core")) * 2 * LAGS, 2 * LAGS)
    give_ref[...] = arrived_ref[:, pl.ds(other, 2 * LAGS), :]


def widen_kernel(arrived_ref, got_ref, ext_ref, wide):
    core = lax.axis_index("core")
    size = CHIPS * 2 * LAGS
    mine = pl.multiple_of(core * 2 * LAGS, 2 * LAGS)
    wide[core] = arrived_ref[:, pl.ds(mine, 2 * LAGS), :].astype(F32).reshape(size, LANES)
    wide[1 - core] = got_ref[...].astype(F32).reshape(size, LANES)
    total = LAGS * LANES
    lane = iota((4 * CHIPS, LANES), 1)
    for b in range(LAGS):
        halves = [wide[c, pl.ds(b, 2 * CHIPS, stride=LAGS), :].reshape(CHIPS // 4, 1, 8, LANES) for c in range(2)]
        plane = jnp.concatenate(halves, axis=1).reshape(4 * CHIPS, LANES)
        ext_ref[:, b * LANES : (b + 1) * LANES] = plane.astype(BF16)
        moved = jnp.where(
            lane < LANES - LAGS, pltpu.roll(plane, LANES - LAGS, 1), pltpu.roll(plane, LANES - LAGS - 1, 1)
        )
        moved = jnp.where(lane == LANES - 1, 0.0, moved)
        ext_ref[:, total + b * LANES : total + (b + 1) * LANES] = moved.astype(BF16)


def correlate_kernel(own, ext_ref, ref_ref, *rest):
    out_hbm, wide, refs, sums, sem = rest[-5:]
    core = lax.axis_index("core")
    side = core if own else 1 - core
    total = LAGS * LANES
    count = 2 * CHIPS
    wide[...] = ref_ref[...].astype(F32).reshape(wide.shape)
    refs[:count, total:] = jnp.zeros((count, LANES), BF16)
    refs[count:, :LANES] = jnp.zeros((count, LANES), BF16)
    for s in range(2):
        for b in range(LAGS):
            plane = wide[pl.ds(s * LAGS + b, CHIPS, stride=2 * LAGS), :].astype(BF16)
            for h in range(2):
                at = h * count + s * CHIPS
                refs[at : at + CHIPS, (b + h) * LANES : (b + h + 1) * LANES] = plane
    rows = ext_ref.shape[0]
    copies = []
    lag = 1
    for pairs in (4, 2, 1, 1):
        windows = [ext_ref[:, pl.ds((lag + 2 * i) * LANES, total + LANES)] for i in range(pairs)]
        part = dot_nt(jnp.concatenate(windows, axis=0), refs[...]) * (1.0 / math.sqrt(total))
        for i in range(pairs):
            for h in range(2):
                at = lag - 1 + 2 * i + h
                sums[:, at * count : (at + 1) * count] = part[i * rows : (i + 1) * rows, h * count : (h + 1) * count]
                column = pl.multiple_of(at * 2 * count + side * count, count)
                copy = pltpu.make_async_copy(
                    sums.at[:, pl.ds(at * count, count)], out_hbm.at[0, :, pl.ds(column, count)], sem.at[at]
                )
                copy.start()
                copies.append(copy)
        lag += 2 * pairs
    for copy in copies:
        copy.wait()


def correlate(own, ext, refs, *out):
    total = LAGS * LANES
    return pl.pallas_call(
        lambda *args: correlate_kernel(own, *args),
        out_shape=jax.ShapeDtypeStruct((1, 4 * CHIPS, LAGS * NREF), F32),
        in_specs=[VMEM, VMEM] + [HBM] * len(out),
        out_specs=HBM,
        scratch_shapes=[
            pltpu.VMEM((CHIPS * 2 * LAGS, LANES), F32),
            pltpu.VMEM((NREF, total + LANES), BF16),
            pltpu.VMEM((4 * CHIPS, total), F32),
            pltpu.SemaphoreType.DMA((LAGS,)),
        ],
        input_output_aliases={2: 0} if out else {},
        compiler_params=params(24),
        cost_estimate=pl.CostEstimate(flops=2_400_000_000, bytes_accessed=4_000_000, transcendentals=0),
        name="correlate_own" if own else "correlate_other",
    )(ext, refs, *out)


def swap_cores(x):
    return lax.ppermute(x, "core", [(0, 1), (1, 0)])


def on_device(raw, taps, row_channel, ref_channel, owner_of_row):
    rows_dev, samples = raw.shape
    total = samples // STRIDE
    window = BLOCK * STRIDE + 2 * HALO
    half = jax.ShapeDtypeStruct((CHIPS, 2 * LAGS, LANES), BF16)
    ids = row_channel.reshape(-1, LANES)
    dec, keep, give = pl.pallas_call(
        decimate_kernel,
        out_shape=(jax.ShapeDtypeStruct((rows_dev, total), BF16), half, half),
        in_specs=[HBM] * 4,
        out_specs=(HBM, HBM, HBM),
        scratch_shapes=[
            pltpu.VMEM((rows_dev, samples + 2 * HALO), BF16),
            pltpu.VMEM((1, TAPS), BF16),
            pltpu.VMEM(ids.shape, jnp.int32),
            pltpu.VMEM((1, NREF), jnp.int32),
            pltpu.VMEM((8, window), F32),
            pltpu.VMEM((rows_dev, total), F32),
            pltpu.VMEM((rows_dev, total), BF16),
            pltpu.VMEM((2, CHIPS * 2 * LAGS, LANES), F32),
            pltpu.VMEM(half.shape, BF16),
            pltpu.VMEM(half.shape, BF16),
            pltpu.SemaphoreType.DMA((4,)),
            pltpu.SemaphoreType.DMA((3,)),
            pltpu.SemaphoreType.DMA((3,)),
        ],
        compiler_params=params(54),
        name="decimate",
    )(raw, taps.reshape(1, TAPS), ids, ref_channel.reshape(1, NREF))
    got = swap_cores(give)
    packet_shape = jax.ShapeDtypeStruct((CHIPS, 6 * LAGS, LANES), BF16)
    packet = pl.pallas_call(
        route_kernel,
        out_shape=packet_shape,
        in_specs=[HBM, VMEM],
        out_specs=VMEM,
        scratch_shapes=[
            pltpu.VMEM((rows_dev, total), BF16),
            pltpu.VMEM((CHIPS * 4 * LAGS, LANES), F32),
            pltpu.SemaphoreType.DMA,
        ],
        compiler_params=params(),
        cost_estimate=pl.CostEstimate(flops=100_000_000, bytes_accessed=4_000_000, transcendentals=0),
        name="route",
    )(dec, owner_of_row.reshape(1, rows_dev))
    packet = pl.pallas_call(
        add_refs_kernel,
        out_shape=packet_shape,
        in_specs=[VMEM] * 3,
        out_specs=VMEM,
        input_output_aliases={0: 0},
        compiler_params=params(),
        name="add_refs",
    )(packet, keep, got)
    arrived = lax.all_to_all(packet, SAME, 0, 0, tiled=True)
    spread = pl.pallas_call(
        spread_kernel,
        out_shape=half,
        in_specs=[VMEM],
        out_specs=VMEM,
        compiler_params=params(),
        name="spread",
    )(arrived)
    rows_give = pl.pallas_call(
        give_kernel,
        out_shape=half,
        in_specs=[VMEM],
        out_specs=VMEM,
        compiler_params=params(),
        name="give",
    )(arrived)
    refs_own = lax.all_to_all(spread, SAME, 0, 0, tiled=True)
    rows_got = swap_cores(rows_give)
    ext = pl.pallas_call(
        widen_kernel,
        out_shape=jax.ShapeDtypeStruct((4 * CHIPS, 2 * total), BF16),
        in_specs=[VMEM, VMEM],
        out_specs=VMEM,
        scratch_shapes=[pltpu.VMEM((2, CHIPS * 2 * LAGS, LANES), F32)],
        compiler_params=params(),
        name="widen",
    )(arrived, rows_got)
    refs_other = swap_cores(refs_own)
    out = correlate(True, ext, refs_own)
    return correlate(False, ext, refs_other, out)


def solution(mesh):
    parts = Mesh(mesh.devices.reshape(4, 4, 2, 4), AXES)
    return jax.shard_map(
        on_device,
        mesh=parts,
        in_specs=(P(AXES, None), P(), P(), P(), P(AXES, None)),
        out_specs=P(AXES, None, None),
        check_vma=False,
    )
```

```python
import math

import jax
import jax.numpy as jnp
from jax import lax
from jax.experimental import pallas as pl
from jax.experimental.pallas import tpu as pltpu
from jax.sharding import Mesh
from jax.sharding import PartitionSpec as P

LAGS = 16
TAPS = 127
STRIDE = 8
NREF = 256
LANES = 128
BLOCK = 128
HALO = 128
CHIPS = 64
LAG_STEPS = (3, 5, 4, 2, 2)
AXES = ("x", "z", "core", "chan")
SAME = ("x", "z", "chan")
NT = (((1,), (1,)), ((), ()))
VMEM = pl.BlockSpec(memory_space=pltpu.VMEM)
HBM = pl.BlockSpec(memory_space=pltpu.HBM)
F32, BF16 = jnp.float32, jnp.bfloat16


def dot_nt(a, b):
    return lax.dot_general(a, b, NT, preferred_element_type=F32)


def params(mib=48):
    return pltpu.CompilerParams(vmem_limit_bytes=mib << 20)


def iota(shape, dim):
    return lax.broadcasted_iota(jnp.int32, shape, dim)


def decimate_kernel(raw_hbm, taps_hbm, ids_hbm, refch_hbm, dec_ref, keep_ref, give_ref,
                    raw, taps, ids, refch, line, dec, stage, raw_sem, small_sem):
    rows = dec_ref.shape[0]
    groups = raw_sem.shape[0]
    chunk = BLOCK * STRIDE
    window = chunk + 2 * HALO
    span = raw_hbm.shape[1] // groups
    loads = [
        pltpu.make_async_copy(
            raw_hbm.at[:, pl.ds(m * span, span)], raw.at[:, pl.ds(HALO + m * span, span)], raw_sem.at[m]
        )
        for m in range(groups)
    ]
    small = [
        pltpu.make_async_copy(taps_hbm, taps, small_sem.at[0]),
        pltpu.make_async_copy(ids_hbm, ids, small_sem.at[1]),
        pltpu.make_async_copy(refch_hbm, refch, small_sem.at[2]),
    ]
    for copy in small + loads:
        copy.start()
    core = lax.axis_index("core")
    own = lax.axis_index(AXES)
    raw[:, :HALO] = jnp.zeros((rows, HALO), BF16)
    raw[:, raw.shape[1] - HALO :] = jnp.zeros((rows, HALO), BF16)
    line[...] = jnp.zeros_like(line)
    small[0].wait()
    line[0:1, 0:TAPS] = taps[...].astype(F32)
    band = pltpu.roll(
        jnp.broadcast_to(line[0:1, :], (BLOCK, window)), HALO - TAPS // 2, 1, stride=STRIDE, stride_axis=0
    )
    band = jnp.transpose(band).astype(BF16)
    small[1].wait()
    small[2].wait()
    at = own * rows
    line0 = at // LANES
    line1 = jnp.minimum(line0 + 1, ids.shape[0] - 1)
    turn = LANES - (at - line0 * LANES)
    pair = [
        pltpu.roll(jnp.broadcast_to(ids[pl.ds(i, 1), :], (8, LANES)), turn, 1) for i in (line0, line1)
    ]
    mine = jnp.where(iota((8, LANES), 1) < turn, pair[0], pair[1])[0:1, :rows]
    refcol = jnp.transpose(jnp.broadcast_to(refch[...], (LANES, NREF)))[:, :rows]
    select = jnp.where(refcol == mine, 1.0, 0.0).astype(BF16)
    per = span // chunk
    loads[0].wait()
    for m in range(groups):
        if m + 1 < groups:
            loads[m + 1].wait()
        windows = [raw[:, pl.ds((m * per + i) * chunk, window)] for i in range(per)]
        part = jnp.dot(jnp.concatenate(windows, axis=0), band, preferred_element_type=F32).astype(BF16)
        for i in range(per):
            at = (m * per + i) * LANES
            dec[:, at : at + LANES] = part[i * rows : (i + 1) * rows].astype(F32)
    lane = iota((16, LANES), 1)
    for r in range(0, rows, 16):
        pieces = [dec[r : r + 16, m * LANES : (m + 1) * LANES] for m in range(LAGS)]
        for k in (1, 2, 4, 8):
            low = (lane & k) == 0
            for t in range(LAGS):
                if not t & k:
                    x, y = pieces[t], pieces[t | k]
                    pieces[t] = jnp.where(low, x, pltpu.roll(y, k, 1))
                    pieces[t | k] = jnp.where(low, pltpu.roll(x, LANES - k, 1), y)
        for b in range(LAGS):
            dec_ref[r : r + 16, b * LANES : (b + 1) * LANES] = pieces[b].astype(BF16)
    for b in range(0, LAGS, 2):
        picked = jnp.dot(select, dec_ref[:, b * LANES : (b + 2) * LANES], preferred_element_type=F32)
        for g in range(4):
            for h in range(2):
                stage[g // 2, pl.ds((g % 2) * LAGS + b + h, CHIPS, stride=2 * LAGS), :] = picked[
                    g * CHIPS : (g + 1) * CHIPS, h * LANES : (h + 1) * LANES
                ]
    shape = (CHIPS, 2 * LAGS, LANES)
    keep_ref[...] = stage[core].astype(BF16).reshape(shape)
    give_ref[...] = stage[1 - core].astype(BF16).reshape(shape)


def route_kernel(dec_ref, owner_ref, packet_ref, stage):
    rows = owner_ref.shape[1]
    owner = owner_ref[...]
    chip = iota((CHIPS, rows), 0)
    before = (iota((rows, rows), 0) < iota((rows, rows), 1)).astype(BF16)
    parts = []
    for core in range(2):
        device = (chip // 4) * 8 + core * 4 + chip % 4
        one = jnp.where(device == owner, 1.0, 0.0)
        rank = jnp.dot(one.astype(BF16), before, preferred_element_type=F32)
        first = jnp.where(rank < 0.5, one, 0.0)
        parts += [first, one - first]
    select = jnp.concatenate(parts, axis=0).astype(BF16)
    for b in range(0, LAGS, 2):
        picked = jnp.dot(select, dec_ref[:, b * LANES : (b + 2) * LANES], preferred_element_type=F32)
        for g in range(4):
            for h in range(2):
                stage[pl.ds(g * LAGS + b + h, CHIPS, stride=4 * LAGS), :] = picked[
                    g * CHIPS : (g + 1) * CHIPS, h * LANES : (h + 1) * LANES
                ]
    packet_ref[:, : 4 * LAGS, :] = stage[...].astype(BF16).reshape(CHIPS, 4 * LAGS, LANES)


def add_refs_kernel(packet_in, keep_ref, got_ref, packet_ref):
    del packet_in
    packet_ref[:, 4 * LAGS :, :] = (keep_ref[...].astype(F32) + got_ref[...].astype(F32)).astype(BF16)


def spread_kernel(arrived_ref, spread_ref, give_ref):
    core = lax.axis_index("core")
    total = jnp.sum(arrived_ref[:, 4 * LAGS :, :].astype(F32), axis=0, keepdims=True)
    spread_ref[...] = jnp.broadcast_to(total, spread_ref.shape).astype(BF16)
    other = pl.multiple_of((1 - core) * 2 * LAGS, 2 * LAGS)
    give_ref[...] = arrived_ref[:, pl.ds(other, 2 * LAGS), :]


def widen_kernel(arrived_ref, got_ref, ext_ref, wide):
    core = lax.axis_index("core")
    size = CHIPS * 2 * LAGS
    mine = pl.multiple_of(core * 2 * LAGS, 2 * LAGS)
    wide[core] = arrived_ref[:, pl.ds(mine, 2 * LAGS), :].astype(F32).reshape(size, LANES)
    wide[1 - core] = got_ref[...].astype(F32).reshape(size, LANES)
    total = LAGS * LANES
    lane = iota((4 * CHIPS, LANES), 1)
    for b in range(LAGS):
        halves = [wide[c, pl.ds(b, 2 * CHIPS, stride=LAGS), :].reshape(CHIPS // 4, 1, 8, LANES) for c in range(2)]
        plane = jnp.concatenate(halves, axis=1).reshape(4 * CHIPS, LANES)
        ext_ref[:, b * LANES : (b + 1) * LANES] = plane.astype(BF16)
        moved = jnp.where(
            lane < LANES - LAGS, pltpu.roll(plane, LANES - LAGS, 1), pltpu.roll(plane, LANES - LAGS - 1, 1)
        )
        moved = jnp.where(lane == LANES - 1, 0.0, moved)
        ext_ref[:, total + b * LANES : total + (b + 1) * LANES] = moved.astype(BF16)


def correlate_kernel(ext_ref, own_ref, other_ref, out_hbm, wide, refs, sums, sem):
    total = LAGS * LANES
    size = CHIPS * 2 * LAGS
    core = lax.axis_index("core")
    wide[core] = own_ref[...].astype(F32).reshape(size, LANES)
    wide[1 - core] = other_ref[...].astype(F32).reshape(size, LANES)
    for g in range(4):
        for b in range(LAGS):
            refs[g * CHIPS : (g + 1) * CHIPS, b * LANES : (b + 1) * LANES] = wide[
                g // 2, pl.ds((g % 2) * LAGS + b, CHIPS, stride=2 * LAGS), :
            ].astype(BF16)
    rows = ext_ref.shape[0]
    copies = []
    lag = 1
    for step, per in enumerate(LAG_STEPS):
        windows = [ext_ref[:, pl.ds((lag + i) * LANES, total)] for i in range(per)]
        part = dot_nt(jnp.concatenate(windows, axis=0), refs[...]) * (1.0 / math.sqrt(total))
        for i in range(per):
            sums[:, (lag - 1 + i) * NREF : (lag + i) * NREF] = part[i * rows : (i + 1) * rows]
        span = pl.ds((lag - 1) * NREF, per * NREF)
        copies.append(pltpu.make_async_copy(sums.at[:, span], out_hbm.at[0, :, span], sem.at[step]))
        copies[-1].start()
        lag += per
    for copy in copies:
        copy.wait()


def swap_cores(x):
    return lax.ppermute(x, "core", [(0, 1), (1, 0)])


def on_device(raw, taps, row_channel, ref_channel, owner_of_row):
    rows_dev, samples = raw.shape
    total = samples // STRIDE
    window = BLOCK * STRIDE + 2 * HALO
    half = jax.ShapeDtypeStruct((CHIPS, 2 * LAGS, LANES), BF16)
    ids = row_channel.reshape(-1, LANES)
    dec, keep, give = pl.pallas_call(
        decimate_kernel,
        out_shape=(jax.ShapeDtypeStruct((rows_dev, total), BF16), half, half),
        in_specs=[HBM] * 4,
        out_specs=(VMEM, VMEM, VMEM),
        scratch_shapes=[
            pltpu.VMEM((rows_dev, samples + 2 * HALO), BF16),
            pltpu.VMEM((1, TAPS), BF16),
            pltpu.VMEM(ids.shape, jnp.int32),
            pltpu.VMEM((1, NREF), jnp.int32),
            pltpu.VMEM((8, window), F32),
            pltpu.VMEM((rows_dev, total), F32),
            pltpu.VMEM((2, CHIPS * 2 * LAGS, LANES), F32),
            pltpu.SemaphoreType.DMA((4,)),
            pltpu.SemaphoreType.DMA((3,)),
        ],
        compiler_params=params(54),
        name="decimate",
    )(raw, taps.reshape(1, TAPS), ids, ref_channel.reshape(1, NREF))
    got = swap_cores(give)
    packet_shape = jax.ShapeDtypeStruct((CHIPS, 6 * LAGS, LANES), BF16)
    packet = pl.pallas_call(
        route_kernel,
        out_shape=packet_shape,
        in_specs=[VMEM, VMEM],
        out_specs=VMEM,
        scratch_shapes=[pltpu.VMEM((CHIPS * 4 * LAGS, LANES), F32)],
        compiler_params=params(),
        cost_estimate=pl.CostEstimate(flops=100_000_000, bytes_accessed=4_000_000, transcendentals=0),
        name="route",
    )(dec, owner_of_row.reshape(1, rows_dev))
    packet = pl.pallas_call(
        add_refs_kernel,
        out_shape=packet_shape,
        in_specs=[VMEM] * 3,
        out_specs=VMEM,
        input_output_aliases={0: 0},
        compiler_params=params(),
        name="add_refs",
    )(packet, keep, got)
    arrived = lax.all_to_all(packet, SAME, 0, 0, tiled=True)
    spread, rows_give = pl.pallas_call(
        spread_kernel,
        out_shape=(half, half),
        in_specs=[VMEM],
        out_specs=(VMEM, VMEM),
        compiler_params=params(),
        name="spread",
    )(arrived)
    refs_own = lax.all_to_all(spread, SAME, 0, 0, tiled=True)
    rows_got = swap_cores(rows_give)
    ext = pl.pallas_call(
        widen_kernel,
        out_shape=jax.ShapeDtypeStruct((4 * CHIPS, 2 * total), BF16),
        in_specs=[VMEM, VMEM],
        out_specs=VMEM,
        scratch_shapes=[pltpu.VMEM((2, CHIPS * 2 * LAGS, LANES), F32)],
        compiler_params=params(),
        name="widen",
    )(arrived, rows_got)
    refs_other = swap_cores(refs_own)
    return pl.pallas_call(
        correlate_kernel,
        out_shape=jax.ShapeDtypeStruct((1, 4 * CHIPS, LAGS * NREF), F32),
        in_specs=[VMEM, VMEM, VMEM],
        out_specs=HBM,
        scratch_shapes=[
            pltpu.VMEM((2, CHIPS * 2 * LAGS, LANES), F32),
            pltpu.VMEM((NREF, total), BF16),
            pltpu.VMEM((4 * CHIPS, LAGS * NREF), F32),
            pltpu.SemaphoreType.DMA((len(LAG_STEPS),)),
        ],
        compiler_params=params(24),
        name="correlate",
    )(ext, refs_own, refs_other)


def solution(mesh):
    parts = Mesh(mesh.devices.reshape(4, 4, 2, 4), AXES)
    return jax.shard_map(
        on_device,
        mesh=parts,
        in_specs=(P(AXES, None), P(), P(), P(), P(AXES, None)),
        out_specs=P(AXES, None, None),
        check_vma=False,
    )
```

```python
import math

import jax
import jax.numpy as jnp
from jax import lax
from jax.experimental import pallas as pl
from jax.experimental.pallas import tpu as pltpu
from jax.sharding import Mesh
from jax.sharding import PartitionSpec as P

LAGS = 16
TAPS = 127
STRIDE = 8
NREF = 256
LANES = 128
BLOCK = 128
HALO = 128
CHIPS = 64
LAG_STEPS = (3, 5, 4, 2, 2)
AXES = ("x", "z", "core", "chan")
SAME = ("x", "z", "chan")
NT = (((1,), (1,)), ((), ()))
VMEM = pl.BlockSpec(memory_space=pltpu.VMEM)
HBM = pl.BlockSpec(memory_space=pltpu.HBM)
F32, BF16 = jnp.float32, jnp.bfloat16


def dot_nt(a, b):
    return lax.dot_general(a, b, NT, preferred_element_type=F32)


def params(mib=48):
    return pltpu.CompilerParams(vmem_limit_bytes=mib << 20)


def iota(shape, dim):
    return lax.broadcasted_iota(jnp.int32, shape, dim)


def decimate_kernel(raw_hbm, taps_hbm, ids_hbm, refch_hbm, dec_ref, keep_ref, give_ref,
                    raw, taps, ids, refch, line, band, dec, stage, raw_sem, small_sem):
    rows = dec_ref.shape[0]
    chunk = BLOCK * STRIDE
    window = chunk + 2 * HALO
    load = pltpu.make_async_copy(raw_hbm, raw.at[:, pl.ds(HALO, raw_hbm.shape[1])], raw_sem)
    small = [
        pltpu.make_async_copy(taps_hbm, taps, small_sem.at[0]),
        pltpu.make_async_copy(ids_hbm, ids, small_sem.at[1]),
        pltpu.make_async_copy(refch_hbm, refch, small_sem.at[2]),
    ]
    for copy in small + [load]:
        copy.start()
    core = lax.axis_index("core")
    own = lax.axis_index(AXES)
    raw[:, :HALO] = jnp.zeros((rows, HALO), BF16)
    raw[:, raw.shape[1] - HALO :] = jnp.zeros((rows, HALO), BF16)
    line[...] = jnp.zeros_like(line)
    band[...] = jnp.zeros_like(band)
    small[0].wait()
    line[0:1, 0:TAPS] = taps[...].astype(F32)
    width = line.shape[1]
    first = pltpu.roll(
        jnp.broadcast_to(line[0:1, :], (16, width)), HALO - TAPS // 2, 1, stride=STRIDE, stride_axis=0
    ).astype(BF16)
    for i in range(BLOCK // 16):
        band[16 * i : 16 * (i + 1), LANES * i : LANES * i + width] = first
    small[1].wait()
    small[2].wait()
    at = own * rows
    line0 = at // LANES
    line1 = jnp.minimum(line0 + 1, ids.shape[0] - 1)
    turn = LANES - (at - line0 * LANES)
    pair = [
        pltpu.roll(jnp.broadcast_to(ids[pl.ds(i, 1), :], (8, LANES)), turn, 1) for i in (line0, line1)
    ]
    mine = jnp.where(iota((8, LANES), 1) < turn, pair[0], pair[1])[0:1, :rows]
    refcol = jnp.transpose(jnp.broadcast_to(refch[...], (LANES, NREF)))[:, :rows]
    select = jnp.where(refcol == mine, 1.0, 0.0).astype(BF16)
    load.wait()
    for at in range(0, LAGS, 2):
        windows = [raw[:, pl.ds((at + i) * chunk, window)] for i in range(2)]
        part = dot_nt(jnp.concatenate(windows, axis=0), band[...])
        for i in range(2):
            dec[:, (at + i) * LANES : (at + i + 1) * LANES] = part[i * rows : (i + 1) * rows].astype(BF16)
    lane = iota((16, LANES), 1)
    for r in range(0, rows, 16):
        pieces = [dec[r : r + 16, m * LANES : (m + 1) * LANES] for m in range(LAGS)]
        for k in (1, 2, 4, 8):
            low = (lane & k) == 0
            for t in range(LAGS):
                if not t & k:
                    x, y = pieces[t], pieces[t | k]
                    pieces[t] = jnp.where(low, x, pltpu.roll(y, k, 1))
                    pieces[t | k] = jnp.where(low, pltpu.roll(x, LANES - k, 1), y)
        for b in range(LAGS):
            dec_ref[r : r + 16, b * LANES : (b + 1) * LANES] = pieces[b]
    for b in range(0, LAGS, 2):
        picked = jnp.dot(select, dec_ref[:, b * LANES : (b + 2) * LANES], preferred_element_type=F32)
        for g in range(4):
            for h in range(2):
                stage[g // 2, pl.ds((g % 2) * LAGS + b + h, CHIPS, stride=2 * LAGS), :] = picked[
                    g * CHIPS : (g + 1) * CHIPS, h * LANES : (h + 1) * LANES
                ]
    shape = (CHIPS, 2 * LAGS, LANES)
    keep_ref[...] = stage[core].astype(BF16).reshape(shape)
    give_ref[...] = stage[1 - core].astype(BF16).reshape(shape)


def route_kernel(dec_ref, owner_ref, packet_ref, stage):
    rows = owner_ref.shape[1]
    owner = owner_ref[...]
    chip = iota((CHIPS, rows), 0)
    before = (iota((rows, rows), 0) < iota((rows, rows), 1)).astype(BF16)
    parts = []
    for core in range(2):
        device = (chip // 4) * 8 + core * 4 + chip % 4
        one = jnp.where(device == owner, 1.0, 0.0)
        rank = jnp.dot(one.astype(BF16), before, preferred_element_type=F32)
        first = jnp.where(rank < 0.5, one, 0.0)
        parts += [first, one - first]
    select = jnp.concatenate(parts, axis=0).astype(BF16)
    for b in range(0, LAGS, 2):
        picked = jnp.dot(select, dec_ref[:, b * LANES : (b + 2) * LANES], preferred_element_type=F32)
        for g in range(4):
            for h in range(2):
                stage[pl.ds(g * LAGS + b + h, CHIPS, stride=4 * LAGS), :] = picked[
                    g * CHIPS : (g + 1) * CHIPS, h * LANES : (h + 1) * LANES
                ]
    packet_ref[:, : 4 * LAGS, :] = stage[...].astype(BF16).reshape(CHIPS, 4 * LAGS, LANES)


def add_refs_kernel(packet_in, keep_ref, got_ref, packet_ref):
    del packet_in
    packet_ref[:, 4 * LAGS :, :] = (keep_ref[...].astype(F32) + got_ref[...].astype(F32)).astype(BF16)


def spread_kernel(arrived_ref, spread_ref, give_ref):
    core = lax.axis_index("core")
    total = jnp.sum(arrived_ref[:, 4 * LAGS :, :].astype(F32), axis=0, keepdims=True)
    spread_ref[...] = jnp.broadcast_to(total, spread_ref.shape).astype(BF16)
    other = pl.multiple_of((1 - core) * 2 * LAGS, 2 * LAGS)
    give_ref[...] = arrived_ref[:, pl.ds(other, 2 * LAGS), :]


def widen_kernel(arrived_ref, got_ref, ext_ref, wide):
    core = lax.axis_index("core")
    size = CHIPS * 2 * LAGS
    mine = pl.multiple_of(core * 2 * LAGS, 2 * LAGS)
    wide[core] = arrived_ref[:, pl.ds(mine, 2 * LAGS), :].astype(F32).reshape(size, LANES)
    wide[1 - core] = got_ref[...].astype(F32).reshape(size, LANES)
    total = LAGS * LANES
    lane = iota((4 * CHIPS, LANES), 1)
    for b in range(LAGS):
        halves = [wide[c, pl.ds(b, 2 * CHIPS, stride=LAGS), :].reshape(CHIPS // 4, 1, 8, LANES) for c in range(2)]
        plane = jnp.concatenate(halves, axis=1).reshape(4 * CHIPS, LANES)
        ext_ref[:, b * LANES : (b + 1) * LANES] = plane.astype(BF16)
        moved = jnp.where(
            lane < LANES - LAGS, pltpu.roll(plane, LANES - LAGS, 1), pltpu.roll(plane, LANES - LAGS - 1, 1)
        )
        moved = jnp.where(lane == LANES - 1, 0.0, moved)
        ext_ref[:, total + b * LANES : total + (b + 1) * LANES] = moved.astype(BF16)


def correlate_kernel(ext_ref, own_ref, other_ref, out_hbm, wide, refs, sums, sem):
    total = LAGS * LANES
    size = CHIPS * 2 * LAGS
    core = lax.axis_index("core")
    wide[core] = own_ref[...].astype(F32).reshape(size, LANES)
    wide[1 - core] = other_ref[...].astype(F32).reshape(size, LANES)
    for g in range(4):
        for b in range(LAGS):
            refs[g * CHIPS : (g + 1) * CHIPS, b * LANES : (b + 1) * LANES] = wide[
                g // 2, pl.ds((g % 2) * LAGS + b, CHIPS, stride=2 * LAGS), :
            ].astype(BF16)
    rows = ext_ref.shape[0]
    copies = []
    lag = 1
    for step, per in enumerate(LAG_STEPS):
        windows = [ext_ref[:, pl.ds((lag + i) * LANES, total)] for i in range(per)]
        part = dot_nt(jnp.concatenate(windows, axis=0), refs[...]) * (1.0 / math.sqrt(total))
        for i in range(per):
            sums[:, (lag - 1 + i) * NREF : (lag + i) * NREF] = part[i * rows : (i + 1) * rows]
        span = pl.ds((lag - 1) * NREF, per * NREF)
        copies.append(pltpu.make_async_copy(sums.at[:, span], out_hbm.at[0, :, span], sem.at[step]))
        copies[-1].start()
        lag += per
    for copy in copies:
        copy.wait()


def swap_cores(x):
    return lax.ppermute(x, "core", [(0, 1), (1, 0)])


def on_device(raw, taps, row_channel, ref_channel, owner_of_row):
    rows_dev, samples = raw.shape
    total = samples // STRIDE
    window = BLOCK * STRIDE + 2 * HALO
    half = jax.ShapeDtypeStruct((CHIPS, 2 * LAGS, LANES), BF16)
    ids = row_channel.reshape(-1, LANES)
    dec, keep, give = pl.pallas_call(
        decimate_kernel,
        out_shape=(jax.ShapeDtypeStruct((rows_dev, total), BF16), half, half),
        in_specs=[HBM] * 4,
        out_specs=(VMEM, VMEM, VMEM),
        scratch_shapes=[
            pltpu.VMEM((rows_dev, samples + 2 * HALO), BF16),
            pltpu.VMEM((1, TAPS), BF16),
            pltpu.VMEM(ids.shape, jnp.int32),
            pltpu.VMEM((1, NREF), jnp.int32),
            pltpu.VMEM((8, 3 * LANES), F32),
            pltpu.VMEM((BLOCK, window), BF16),
            pltpu.VMEM((rows_dev, total), BF16),
            pltpu.VMEM((2, CHIPS * 2 * LAGS, LANES), F32),
            pltpu.SemaphoreType.DMA,
            pltpu.SemaphoreType.DMA((3,)),
        ],
        compiler_params=params(54),
        name="decimate",
    )(raw, taps.reshape(1, TAPS), ids, ref_channel.reshape(1, NREF))
    got = swap_cores(give)
    packet_shape = jax.ShapeDtypeStruct((CHIPS, 6 * LAGS, LANES), BF16)
    packet = pl.pallas_call(
        route_kernel,
        out_shape=packet_shape,
        in_specs=[VMEM, VMEM],
        out_specs=VMEM,
        scratch_shapes=[pltpu.VMEM((CHIPS * 4 * LAGS, LANES), F32)],
        compiler_params=params(),
        cost_estimate=pl.CostEstimate(flops=100_000_000, bytes_accessed=4_000_000, transcendentals=0),
        name="route",
    )(dec, owner_of_row.reshape(1, rows_dev))
    packet = pl.pallas_call(
        add_refs_kernel,
        out_shape=packet_shape,
        in_specs=[VMEM] * 3,
        out_specs=VMEM,
        input_output_aliases={0: 0},
        compiler_params=params(),
        name="add_refs",
    )(packet, keep, got)
    arrived = lax.all_to_all(packet, SAME, 0, 0, tiled=True)
    spread, rows_give = pl.pallas_call(
        spread_kernel,
        out_shape=(half, half),
        in_specs=[VMEM],
        out_specs=(VMEM, VMEM),
        compiler_params=params(),
        name="spread",
    )(arrived)
    refs_own = lax.all_to_all(spread, SAME, 0, 0, tiled=True)
    rows_got = swap_cores(rows_give)
    ext = pl.pallas_call(
        widen_kernel,
        out_shape=jax.ShapeDtypeStruct((4 * CHIPS, 2 * total), BF16),
        in_specs=[VMEM, VMEM],
        out_specs=VMEM,
        scratch_shapes=[pltpu.VMEM((2, CHIPS * 2 * LAGS, LANES), F32)],
        compiler_params=params(),
        name="widen",
    )(arrived, rows_got)
    refs_other = swap_cores(refs_own)
    return pl.pallas_call(
        correlate_kernel,
        out_shape=jax.ShapeDtypeStruct((1, 4 * CHIPS, LAGS * NREF), F32),
        in_specs=[VMEM, VMEM, VMEM],
        out_specs=HBM,
        scratch_shapes=[
            pltpu.VMEM((2, CHIPS * 2 * LAGS, LANES), F32),
            pltpu.VMEM((NREF, total), BF16),
            pltpu.VMEM((4 * CHIPS, LAGS * NREF), F32),
            pltpu.SemaphoreType.DMA((len(LAG_STEPS),)),
        ],
        compiler_params=params(24),
        name="correlate",
    )(ext, refs_own, refs_other)


def solution(mesh):
    parts = Mesh(mesh.devices.reshape(4, 4, 2, 4), AXES)
    return jax.shard_map(
        on_device,
        mesh=parts,
        in_specs=(P(AXES, None), P(), P(), P(), P(AXES, None)),
        out_specs=P(AXES, None, None),
        check_vma=False,
    )
```

```python
import math

import jax
import jax.numpy as jnp
from jax import lax
from jax.experimental import pallas as pl
from jax.experimental.pallas import tpu as pltpu
from jax.sharding import Mesh
from jax.sharding import PartitionSpec as P

LAGS = 16
TAPS = 127
STRIDE = 8
NREF = 256
LANES = 128
BLOCK = 128
HALO = 128
CHIPS = 64
LAG_STEPS = (3, 5, 4, 2, 2)
AXES = ("x", "z", "core", "chan")
SAME = ("x", "z", "chan")
NT = (((1,), (1,)), ((), ()))
VMEM = pl.BlockSpec(memory_space=pltpu.VMEM)
HBM = pl.BlockSpec(memory_space=pltpu.HBM)
F32, BF16 = jnp.float32, jnp.bfloat16


def dot_nt(a, b):
    return lax.dot_general(a, b, NT, preferred_element_type=F32)


def params(mib=48):
    return pltpu.CompilerParams(vmem_limit_bytes=mib << 20)


def iota(shape, dim):
    return lax.broadcasted_iota(jnp.int32, shape, dim)


def decimate_kernel(raw_hbm, taps, dec_ref, raw, line, band, dec, sem):
    rows = dec_ref.shape[0]
    chunk = BLOCK * STRIDE
    window = chunk + 2 * HALO
    load = pltpu.make_async_copy(raw_hbm, raw.at[:, pl.ds(HALO, raw_hbm.shape[1])], sem)
    load.start()
    raw[:, :HALO] = jnp.zeros((rows, HALO), BF16)
    raw[:, raw.shape[1] - HALO :] = jnp.zeros((rows, HALO), BF16)
    line[...] = jnp.zeros_like(line)
    band[...] = jnp.zeros_like(band)
    line[0:1, 0:TAPS] = taps[...].astype(F32)
    width = line.shape[1]
    first = pltpu.roll(
        jnp.broadcast_to(line[0:1, :], (16, width)), HALO - TAPS // 2, 1, stride=STRIDE, stride_axis=0
    ).astype(BF16)
    for i in range(BLOCK // 16):
        band[16 * i : 16 * (i + 1), LANES * i : LANES * i + width] = first
    load.wait()
    for at in range(0, LAGS, 2):
        windows = [raw[:, pl.ds((at + i) * chunk, window)] for i in range(2)]
        part = dot_nt(jnp.concatenate(windows, axis=0), band[...])
        for i in range(2):
            dec[:, (at + i) * LANES : (at + i + 1) * LANES] = part[i * rows : (i + 1) * rows].astype(BF16)
    lane = iota((16, LANES), 1)
    for r in range(0, rows, 16):
        pieces = [dec[r : r + 16, m * LANES : (m + 1) * LANES] for m in range(LAGS)]
        for k in (1, 2, 4, 8):
            low = (lane & k) == 0
            for t in range(LAGS):
                if not t & k:
                    x, y = pieces[t], pieces[t | k]
                    pieces[t] = jnp.where(low, x, pltpu.roll(y, k, 1))
                    pieces[t | k] = jnp.where(low, pltpu.roll(x, LANES - k, 1), y)
        for b in range(LAGS):
            dec_ref[r : r + 16, b * LANES : (b + 1) * LANES] = pieces[b]


def pick_kernel(dec_ref, ids, refch, keep_ref, give_ref, stage):
    rows = dec_ref.shape[0]
    core = lax.axis_index("core")
    own = lax.axis_index(AXES)
    at = own * rows
    line0 = at // LANES
    line1 = jnp.minimum(line0 + 1, ids.shape[0] - 1)
    turn = LANES - (at - line0 * LANES)
    pair = [
        pltpu.roll(jnp.broadcast_to(ids[pl.ds(i, 1), :], (8, LANES)), turn, 1) for i in (line0, line1)
    ]
    mine = jnp.where(iota((8, LANES), 1) < turn, pair[0], pair[1])[0:1, :rows]
    refcol = jnp.transpose(jnp.broadcast_to(refch[...], (LANES, NREF)))[:, :rows]
    select = jnp.where(refcol == mine, 1.0, 0.0).astype(BF16)
    for b in range(0, LAGS, 2):
        picked = jnp.dot(select, dec_ref[:, b * LANES : (b + 2) * LANES], preferred_element_type=F32)
        for g in range(4):
            for h in range(2):
                stage[g // 2, pl.ds((g % 2) * LAGS + b + h, CHIPS, stride=2 * LAGS), :] = picked[
                    g * CHIPS : (g + 1) * CHIPS, h * LANES : (h + 1) * LANES
                ]
    shape = (CHIPS, 2 * LAGS, LANES)
    keep_ref[...] = stage[core].astype(BF16).reshape(shape)
    give_ref[...] = stage[1 - core].astype(BF16).reshape(shape)


def route_kernel(dec_ref, owner_ref, packet_ref, stage):
    rows = owner_ref.shape[1]
    owner = owner_ref[...]
    chip = iota((CHIPS, rows), 0)
    before = (iota((rows, rows), 0) < iota((rows, rows), 1)).astype(BF16)
    parts = []
    for core in range(2):
        device = (chip // 4) * 8 + core * 4 + chip % 4
        one = jnp.where(device == owner, 1.0, 0.0)
        rank = jnp.dot(one.astype(BF16), before, preferred_element_type=F32)
        first = jnp.where(rank < 0.5, one, 0.0)
        parts += [first, one - first]
    select = jnp.concatenate(parts, axis=0).astype(BF16)
    for b in range(0, LAGS, 2):
        picked = jnp.dot(select, dec_ref[:, b * LANES : (b + 2) * LANES], preferred_element_type=F32)
        for g in range(4):
            for h in range(2):
                stage[pl.ds(g * LAGS + b + h, CHIPS, stride=4 * LAGS), :] = picked[
                    g * CHIPS : (g + 1) * CHIPS, h * LANES : (h + 1) * LANES
                ]
    packet_ref[:, : 4 * LAGS, :] = stage[...].astype(BF16).reshape(CHIPS, 4 * LAGS, LANES)


def add_refs_kernel(packet_in, keep_ref, got_ref, packet_ref):
    del packet_in
    packet_ref[:, 4 * LAGS :, :] = (keep_ref[...].astype(F32) + got_ref[...].astype(F32)).astype(BF16)


def spread_kernel(arrived_ref, spread_ref, give_ref):
    core = lax.axis_index("core")
    total = jnp.sum(arrived_ref[:, 4 * LAGS :, :].astype(F32), axis=0, keepdims=True)
    spread_ref[...] = jnp.broadcast_to(total, spread_ref.shape).astype(BF16)
    other = pl.multiple_of((1 - core) * 2 * LAGS, 2 * LAGS)
    give_ref[...] = arrived_ref[:, pl.ds(other, 2 * LAGS), :]


def widen_kernel(arrived_ref, got_ref, ext_ref, wide):
    core = lax.axis_index("core")
    size = CHIPS * 2 * LAGS
    mine = pl.multiple_of(core * 2 * LAGS, 2 * LAGS)
    wide[core] = arrived_ref[:, pl.ds(mine, 2 * LAGS), :].astype(F32).reshape(size, LANES)
    wide[1 - core] = got_ref[...].astype(F32).reshape(size, LANES)
    total = LAGS * LANES
    lane = iota((4 * CHIPS, LANES), 1)
    for b in range(LAGS):
        halves = [wide[c, pl.ds(b, 2 * CHIPS, stride=LAGS), :].reshape(CHIPS // 4, 1, 8, LANES) for c in range(2)]
        plane = jnp.concatenate(halves, axis=1).reshape(4 * CHIPS, LANES)
        ext_ref[:, b * LANES : (b + 1) * LANES] = plane.astype(BF16)
        moved = jnp.where(
            lane < LANES - LAGS, pltpu.roll(plane, LANES - LAGS, 1), pltpu.roll(plane, LANES - LAGS - 1, 1)
        )
        moved = jnp.where(lane == LANES - 1, 0.0, moved)
        ext_ref[:, total + b * LANES : total + (b + 1) * LANES] = moved.astype(BF16)


def correlate_kernel(ext_ref, own_ref, other_ref, out_hbm, wide, refs, sums, sem):
    total = LAGS * LANES
    size = CHIPS * 2 * LAGS
    core = lax.axis_index("core")
    wide[core] = own_ref[...].astype(F32).reshape(size, LANES)
    wide[1 - core] = other_ref[...].astype(F32).reshape(size, LANES)
    for g in range(4):
        for b in range(LAGS):
            refs[g * CHIPS : (g + 1) * CHIPS, b * LANES : (b + 1) * LANES] = wide[
                g // 2, pl.ds((g % 2) * LAGS + b, CHIPS, stride=2 * LAGS), :
            ].astype(BF16)
    rows = ext_ref.shape[0]
    copies = []
    lag = 1
    for step, per in enumerate(LAG_STEPS):
        windows = [ext_ref[:, pl.ds((lag + i) * LANES, total)] for i in range(per)]
        part = dot_nt(jnp.concatenate(windows, axis=0), refs[...]) * (1.0 / math.sqrt(total))
        for i in range(per):
            sums[:, (lag - 1 + i) * NREF : (lag + i) * NREF] = part[i * rows : (i + 1) * rows]
        span = pl.ds((lag - 1) * NREF, per * NREF)
        copies.append(pltpu.make_async_copy(sums.at[:, span], out_hbm.at[0, :, span], sem.at[step]))
        copies[-1].start()
        lag += per
    for copy in copies:
        copy.wait()


def swap_cores(x):
    return lax.ppermute(x, "core", [(0, 1), (1, 0)])


def on_device(raw, taps, row_channel, ref_channel, owner_of_row):
    rows_dev, samples = raw.shape
    total = samples // STRIDE
    window = BLOCK * STRIDE + 2 * HALO
    half = jax.ShapeDtypeStruct((CHIPS, 2 * LAGS, LANES), BF16)
    ids = row_channel.reshape(-1, LANES)
    dec = pl.pallas_call(
        decimate_kernel,
        out_shape=jax.ShapeDtypeStruct((rows_dev, total), BF16),
        in_specs=[HBM, VMEM],
        out_specs=VMEM,
        scratch_shapes=[
            pltpu.VMEM((rows_dev, samples + 2 * HALO), BF16),
            pltpu.VMEM((8, 3 * LANES), F32),
            pltpu.VMEM((BLOCK, window), BF16),
            pltpu.VMEM((rows_dev, total), BF16),
            pltpu.SemaphoreType.DMA,
        ],
        compiler_params=params(52),
        name="decimate",
    )(raw, taps.reshape(1, TAPS))
    keep, give = pl.pallas_call(
        pick_kernel,
        out_shape=(half, half),
        in_specs=[VMEM] * 3,
        out_specs=(VMEM, VMEM),
        scratch_shapes=[pltpu.VMEM((2, CHIPS * 2 * LAGS, LANES), F32)],
        compiler_params=params(),
        name="pick",
    )(dec, ids, ref_channel.reshape(1, NREF))
    got = swap_cores(give)
    packet_shape = jax.ShapeDtypeStruct((CHIPS, 6 * LAGS, LANES), BF16)
    packet = pl.pallas_call(
        route_kernel,
        out_shape=packet_shape,
        in_specs=[VMEM, VMEM],
        out_specs=VMEM,
        scratch_shapes=[pltpu.VMEM((CHIPS * 4 * LAGS, LANES), F32)],
        compiler_params=params(),
        cost_estimate=pl.CostEstimate(flops=100_000_000, bytes_accessed=4_000_000, transcendentals=0),
        name="route",
    )(dec, owner_of_row.reshape(1, rows_dev))
    packet = pl.pallas_call(
        add_refs_kernel,
        out_shape=packet_shape,
        in_specs=[VMEM] * 3,
        out_specs=VMEM,
        input_output_aliases={0: 0},
        compiler_params=params(),
        name="add_refs",
    )(packet, keep, got)
    arrived = lax.all_to_all(packet, SAME, 0, 0, tiled=True)
    spread, rows_give = pl.pallas_call(
        spread_kernel,
        out_shape=(half, half),
        in_specs=[VMEM],
        out_specs=(VMEM, VMEM),
        compiler_params=params(),
        name="spread",
    )(arrived)
    refs_own = lax.all_to_all(spread, SAME, 0, 0, tiled=True)
    rows_got = swap_cores(rows_give)
    ext = pl.pallas_call(
        widen_kernel,
        out_shape=jax.ShapeDtypeStruct((4 * CHIPS, 2 * total), BF16),
        in_specs=[VMEM, VMEM],
        out_specs=VMEM,
        scratch_shapes=[pltpu.VMEM((2, CHIPS * 2 * LAGS, LANES), F32)],
        compiler_params=params(),
        name="widen",
    )(arrived, rows_got)
    refs_other = swap_cores(refs_own)
    return pl.pallas_call(
        correlate_kernel,
        out_shape=jax.ShapeDtypeStruct((1, 4 * CHIPS, LAGS * NREF), F32),
        in_specs=[VMEM, VMEM, VMEM],
        out_specs=HBM,
        scratch_shapes=[
            pltpu.VMEM((2, CHIPS * 2 * LAGS, LANES), F32),
            pltpu.VMEM((NREF, total), BF16),
            pltpu.VMEM((4 * CHIPS, LAGS * NREF), F32),
            pltpu.SemaphoreType.DMA((len(LAG_STEPS),)),
        ],
        compiler_params=params(24),
        name="correlate",
    )(ext, refs_own, refs_other)


def solution(mesh):
    parts = Mesh(mesh.devices.reshape(4, 4, 2, 4), AXES)
    return jax.shard_map(
        on_device,
        mesh=parts,
        in_specs=(P(AXES, None), P(), P(), P(), P(AXES, None)),
        out_specs=P(AXES, None, None),
        check_vma=False,
    )
```

```python
import math

import jax
import jax.numpy as jnp
from jax import lax
from jax.experimental import pallas as pl
from jax.experimental.pallas import tpu as pltpu
from jax.sharding import Mesh
from jax.sharding import PartitionSpec as P

LAGS = 16
TAPS = 127
STRIDE = 8
NREF = 256
LANES = 128
BLOCK = 128
HALO = 128
CHIPS = 64
LAG_STEPS = (3, 5, 4, 2, 2)
AXES = ("x", "z", "core", "chan")
SAME = ("x", "z", "chan")
NT = (((1,), (1,)), ((), ()))
VMEM = pl.BlockSpec(memory_space=pltpu.VMEM)
HBM = pl.BlockSpec(memory_space=pltpu.HBM)
F32, BF16 = jnp.float32, jnp.bfloat16


def dot_nt(a, b):
    return lax.dot_general(a, b, NT, preferred_element_type=F32)


def params(mib=48):
    return pltpu.CompilerParams(vmem_limit_bytes=mib << 20)


def iota(shape, dim):
    return lax.broadcasted_iota(jnp.int32, shape, dim)


def decimate_kernel(raw_hbm, taps, dec_ref, raw, line, band, dec, sem):
    rows = dec_ref.shape[0]
    chunk = BLOCK * STRIDE
    window = chunk + 2 * HALO
    load = pltpu.make_async_copy(raw_hbm, raw.at[:, pl.ds(HALO, raw_hbm.shape[1])], sem)
    load.start()
    raw[:, :HALO] = jnp.zeros((rows, HALO), BF16)
    raw[:, raw.shape[1] - HALO :] = jnp.zeros((rows, HALO), BF16)
    line[...] = jnp.zeros_like(line)
    band[...] = jnp.zeros_like(band)
    line[0:1, 0:TAPS] = taps[...].astype(F32)
    width = line.shape[1]
    first = pltpu.roll(
        jnp.broadcast_to(line[0:1, :], (16, width)), HALO - TAPS // 2, 1, stride=STRIDE, stride_axis=0
    ).astype(BF16)
    for i in range(BLOCK // 16):
        band[16 * i : 16 * (i + 1), LANES * i : LANES * i + width] = first
    load.wait()
    for at in range(0, LAGS, 2):
        windows = [raw[:, pl.ds((at + i) * chunk, window)] for i in range(2)]
        part = dot_nt(jnp.concatenate(windows, axis=0), band[...])
        for i in range(2):
            dec[:, (at + i) * LANES : (at + i + 1) * LANES] = part[i * rows : (i + 1) * rows].astype(BF16)
    lane = iota((16, LANES), 1)
    for r in range(0, rows, 16):
        pieces = [dec[r : r + 16, m * LANES : (m + 1) * LANES] for m in range(LAGS)]
        for k in (1, 2, 4, 8):
            low = (lane & k) == 0
            for t in range(LAGS):
                if not t & k:
                    x, y = pieces[t], pieces[t | k]
                    pieces[t] = jnp.where(low, x, pltpu.roll(y, k, 1))
                    pieces[t | k] = jnp.where(low, pltpu.roll(x, LANES - k, 1), y)
        for b in range(LAGS):
            dec_ref[r : r + 16, b * LANES : (b + 1) * LANES] = pieces[b]


def pick_kernel(dec_ref, ids, refch, keep_ref, give_ref):
    rows = dec_ref.shape[0]
    count = keep_ref.shape[0]
    core = lax.axis_index("core")
    own = lax.axis_index(AXES)
    at = own * rows
    line0 = at // LANES
    line1 = jnp.minimum(line0 + 1, ids.shape[0] - 1)
    turn = LANES - (at - line0 * LANES)
    pair = [
        pltpu.roll(jnp.broadcast_to(ids[pl.ds(i, 1), :], (8, LANES)), turn, 1) for i in (line0, line1)
    ]
    mine = jnp.where(iota((8, LANES), 1) < turn, pair[0], pair[1])[0:1, :rows]
    refcol = jnp.transpose(jnp.broadcast_to(refch[...], (LANES, NREF)))[:, :rows]
    select = jnp.where(refcol == mine, 1.0, 0.0)
    halves = (select[:count], select[count:])
    halves = (jnp.where(core == 0, *halves), jnp.where(core == 0, *halves[::-1]))
    select = jnp.concatenate(halves, axis=0).astype(BF16)
    for b in range(0, LAGS, 2):
        span = slice(b * LANES, (b + 2) * LANES)
        picked = jnp.dot(select, dec_ref[:, span], preferred_element_type=F32).astype(BF16)
        keep_ref[:, span] = picked[:count]
        give_ref[:, span] = picked[count:]


def route_kernel(dec_ref, owner_ref, packet_ref, stage):
    rows = owner_ref.shape[1]
    owner = owner_ref[...]
    chip = iota((CHIPS, rows), 0)
    before = (iota((rows, rows), 0) < iota((rows, rows), 1)).astype(BF16)
    parts = []
    for core in range(2):
        device = (chip // 4) * 8 + core * 4 + chip % 4
        one = jnp.where(device == owner, 1.0, 0.0)
        rank = jnp.dot(one.astype(BF16), before, preferred_element_type=F32)
        first = jnp.where(rank < 0.5, one, 0.0)
        parts += [first, one - first]
    select = jnp.concatenate(parts, axis=0).astype(BF16)
    for b in range(0, LAGS, 2):
        picked = jnp.dot(select, dec_ref[:, b * LANES : (b + 2) * LANES], preferred_element_type=F32)
        for g in range(4):
            for h in range(2):
                stage[pl.ds(g * LAGS + b + h, CHIPS, stride=4 * LAGS), :] = picked[
                    g * CHIPS : (g + 1) * CHIPS, h * LANES : (h + 1) * LANES
                ]
    packet_ref[:, : 4 * LAGS, :] = stage[...].astype(BF16).reshape(CHIPS, 4 * LAGS, LANES)


def add_refs_kernel(packet_in, keep_ref, got_ref, packet_ref, stage):
    del packet_in
    for s in range(2):
        rows = slice(s * CHIPS, (s + 1) * CHIPS)
        for b in range(LAGS):
            lanes = slice(b * LANES, (b + 1) * LANES)
            stage[pl.ds(s * LAGS + b, CHIPS, stride=2 * LAGS), :] = keep_ref[rows, lanes].astype(F32) + got_ref[
                rows, lanes
            ].astype(F32)
    packet_ref[:, 4 * LAGS :, :] = stage[...].astype(BF16).reshape(CHIPS, 2 * LAGS, LANES)


def spread_kernel(arrived_ref, spread_ref, give_ref):
    core = lax.axis_index("core")
    total = jnp.sum(arrived_ref[:, 4 * LAGS :, :].astype(F32), axis=0, keepdims=True)
    spread_ref[...] = jnp.broadcast_to(total, spread_ref.shape).astype(BF16)
    other = pl.multiple_of((1 - core) * 2 * LAGS, 2 * LAGS)
    give_ref[...] = arrived_ref[:, pl.ds(other, 2 * LAGS), :]


def lay_out_refs(refs_ref, wide, write):
    wide[...] = refs_ref[...].astype(F32).reshape(wide.shape)
    for s in range(2):
        for b in range(LAGS):
            write(s * CHIPS, b * LANES, wide[pl.ds(s * LAGS + b, CHIPS, stride=2 * LAGS), :].astype(BF16))


def widen_kernel(arrived_ref, got_ref, own_ref, ext_ref, mine_ref, wide, wide_refs):
    core = lax.axis_index("core")
    size = CHIPS * 2 * LAGS
    mine = pl.multiple_of(core * 2 * LAGS, 2 * LAGS)
    wide[core] = arrived_ref[:, pl.ds(mine, 2 * LAGS), :].astype(F32).reshape(size, LANES)
    wide[1 - core] = got_ref[...].astype(F32).reshape(size, LANES)
    total = LAGS * LANES
    lane = iota((4 * CHIPS, LANES), 1)
    for b in range(LAGS):
        halves = [wide[c, pl.ds(b, 2 * CHIPS, stride=LAGS), :].reshape(CHIPS // 4, 1, 8, LANES) for c in range(2)]
        plane = jnp.concatenate(halves, axis=1).reshape(4 * CHIPS, LANES)
        ext_ref[:, b * LANES : (b + 1) * LANES] = plane.astype(BF16)
        moved = jnp.where(
            lane < LANES - LAGS, pltpu.roll(plane, LANES - LAGS, 1), pltpu.roll(plane, LANES - LAGS - 1, 1)
        )
        moved = jnp.where(lane == LANES - 1, 0.0, moved)
        ext_ref[:, total + b * LANES : total + (b + 1) * LANES] = moved.astype(BF16)

    def write(row, lane, piece):
        mine_ref[row : row + CHIPS, lane : lane + LANES] = piece

    lay_out_refs(own_ref, wide_refs, write)


def correlate_kernel(ext_ref, mine_ref, other_ref, out_hbm, wide, refs, sums, sem):
    total = LAGS * LANES
    core = lax.axis_index("core")
    half = NREF // 2

    def write(row, lane, piece):
        row = pl.multiple_of((1 - core) * half + row, CHIPS)
        refs[pl.ds(row, CHIPS), lane : lane + LANES] = piece

    refs[pl.ds(pl.multiple_of(core * half, half), half), :] = mine_ref[...]
    lay_out_refs(other_ref, wide, write)
    rows = ext_ref.shape[0]
    copies = []
    lag = 1
    for step, per in enumerate(LAG_STEPS):
        windows = [ext_ref[:, pl.ds((lag + i) * LANES, total)] for i in range(per)]
        part = dot_nt(jnp.concatenate(windows, axis=0), refs[...]) * (1.0 / math.sqrt(total))
        for i in range(per):
            sums[:, (lag - 1 + i) * NREF : (lag + i) * NREF] = part[i * rows : (i + 1) * rows]
        span = pl.ds((lag - 1) * NREF, per * NREF)
        copies.append(pltpu.make_async_copy(sums.at[:, span], out_hbm.at[0, :, span], sem.at[step]))
        copies[-1].start()
        lag += per
    for copy in copies:
        copy.wait()


def swap_cores(x):
    return lax.ppermute(x, "core", [(0, 1), (1, 0)])


def on_device(raw, taps, row_channel, ref_channel, owner_of_row):
    rows_dev, samples = raw.shape
    total = samples // STRIDE
    window = BLOCK * STRIDE + 2 * HALO
    half = jax.ShapeDtypeStruct((CHIPS, 2 * LAGS, LANES), BF16)
    plain = jax.ShapeDtypeStruct((NREF // 2, total), BF16)
    ids = row_channel.reshape(-1, LANES)
    dec = pl.pallas_call(
        decimate_kernel,
        out_shape=jax.ShapeDtypeStruct((rows_dev, total), BF16),
        in_specs=[HBM, VMEM],
        out_specs=VMEM,
        scratch_shapes=[
            pltpu.VMEM((rows_dev, samples + 2 * HALO), BF16),
            pltpu.VMEM((8, 3 * LANES), F32),
            pltpu.VMEM((BLOCK, window), BF16),
            pltpu.VMEM((rows_dev, total), BF16),
            pltpu.SemaphoreType.DMA,
        ],
        compiler_params=params(52),
        name="decimate",
    )(raw, taps.reshape(1, TAPS))
    keep, give = pl.pallas_call(
        pick_kernel,
        out_shape=(plain, plain),
        in_specs=[VMEM] * 3,
        out_specs=(VMEM, VMEM),
        compiler_params=params(),
        name="pick",
    )(dec, ids, ref_channel.reshape(1, NREF))
    got = swap_cores(give)
    packet_shape = jax.ShapeDtypeStruct((CHIPS, 6 * LAGS, LANES), BF16)
    packet = pl.pallas_call(
        route_kernel,
        out_shape=packet_shape,
        in_specs=[VMEM, VMEM],
        out_specs=VMEM,
        scratch_shapes=[pltpu.VMEM((CHIPS * 4 * LAGS, LANES), F32)],
        compiler_params=params(),
        cost_estimate=pl.CostEstimate(flops=100_000_000, bytes_accessed=4_000_000, transcendentals=0),
        name="route",
    )(dec, owner_of_row.reshape(1, rows_dev))
    packet = pl.pallas_call(
        add_refs_kernel,
        out_shape=packet_shape,
        in_specs=[VMEM] * 3,
        out_specs=VMEM,
        scratch_shapes=[pltpu.VMEM((CHIPS * 2 * LAGS, LANES), F32)],
        input_output_aliases={0: 0},
        compiler_params=params(),
        name="add_refs",
    )(packet, keep, got)
    arrived = lax.all_to_all(packet, SAME, 0, 0, tiled=True)
    spread, rows_give = pl.pallas_call(
        spread_kernel,
        out_shape=(half, half),
        in_specs=[VMEM],
        out_specs=(VMEM, VMEM),
        compiler_params=params(),
        name="spread",
    )(arrived)
    refs_own = lax.all_to_all(spread, SAME, 0, 0, tiled=True)
    rows_got = swap_cores(rows_give)
    ext, refs_mine = pl.pallas_call(
        widen_kernel,
        out_shape=(jax.ShapeDtypeStruct((4 * CHIPS, 2 * total), BF16), plain),
        in_specs=[VMEM, VMEM, VMEM],
        out_specs=(VMEM, VMEM),
        scratch_shapes=[
            pltpu.VMEM((2, CHIPS * 2 * LAGS, LANES), F32),
            pltpu.VMEM((CHIPS * 2 * LAGS, LANES), F32),
        ],
        compiler_params=params(),
        name="widen",
    )(arrived, rows_got, refs_own)
    refs_other = swap_cores(refs_own)
    return pl.pallas_call(
        correlate_kernel,
        out_shape=jax.ShapeDtypeStruct((1, 4 * CHIPS, LAGS * NREF), F32),
        in_specs=[VMEM, VMEM, VMEM],
        out_specs=HBM,
        scratch_shapes=[
            pltpu.VMEM((CHIPS * 2 * LAGS, LANES), F32),
            pltpu.VMEM((NREF, total), BF16),
            pltpu.VMEM((4 * CHIPS, LAGS * NREF), F32),
            pltpu.SemaphoreType.DMA((len(LAG_STEPS),)),
        ],
        compiler_params=params(24),
        name="correlate",
    )(ext, refs_mine, refs_other)


def solution(mesh):
    parts = Mesh(mesh.devices.reshape(4, 4, 2, 4), AXES)
    return jax.shard_map(
        on_device,
        mesh=parts,
        in_specs=(P(AXES, None), P(), P(), P(), P(AXES, None)),
        out_specs=P(AXES, None, None),
        check_vma=False,
    )
```

```python
import math

import jax
import jax.numpy as jnp
from jax import lax
from jax.experimental import pallas as pl
from jax.experimental.pallas import tpu as pltpu
from jax.sharding import Mesh
from jax.sharding import PartitionSpec as P

LAGS = 16
TAPS = 127
STRIDE = 8
NREF = 256
LANES = 128
BLOCK = 128
HALO = 128
CHIPS = 64
PAD = 8
LAG_STEPS = (3, 5, 4, 2, 2)
AXES = ("x", "z", "core", "chan")
SAME = ("x", "z", "chan")
NT = (((1,), (1,)), ((), ()))
VMEM = pl.BlockSpec(memory_space=pltpu.VMEM)
HBM = pl.BlockSpec(memory_space=pltpu.HBM)
F32, BF16 = jnp.float32, jnp.bfloat16


def dot_nt(a, b):
    return lax.dot_general(a, b, NT, preferred_element_type=F32)


def params(mib=48):
    return pltpu.CompilerParams(vmem_limit_bytes=mib << 20)


def iota(shape, dim):
    return lax.broadcasted_iota(jnp.int32, shape, dim)


def decimate_kernel(raw_hbm, taps, dec_ref, raw, line, band, dec, sem):
    rows = dec_ref.shape[0]
    chunk = BLOCK * STRIDE
    window = chunk + 2 * HALO
    load = pltpu.make_async_copy(raw_hbm, raw.at[:, pl.ds(HALO, raw_hbm.shape[1])], sem)
    load.start()
    raw[:, :HALO] = jnp.zeros((rows, HALO), BF16)
    raw[:, raw.shape[1] - HALO :] = jnp.zeros((rows, HALO), BF16)
    line[...] = jnp.zeros_like(line)
    band[...] = jnp.zeros_like(band)
    line[0:1, 0:TAPS] = taps[...].astype(F32)
    width = line.shape[1]
    first = pltpu.roll(
        jnp.broadcast_to(line[0:1, :], (16, width)), HALO - TAPS // 2, 1, stride=STRIDE, stride_axis=0
    ).astype(BF16)
    for i in range(BLOCK // 16):
        band[16 * i : 16 * (i + 1), LANES * i : LANES * i + width] = first
    load.wait()
    for at in range(0, LAGS, 2):
        windows = [raw[:, pl.ds((at + i) * chunk, window)] for i in range(2)]
        part = dot_nt(jnp.concatenate(windows, axis=0), band[...])
        for i in range(2):
            dec[:, (at + i) * LANES : (at + i + 1) * LANES] = part[i * rows : (i + 1) * rows].astype(BF16)
    lane = iota((16, LANES), 1)
    for r in range(0, rows, 16):
        pieces = [dec[r : r + 16, m * LANES : (m + 1) * LANES] for m in range(LAGS)]
        for k in (1, 2, 4, 8):
            low = (lane & k) == 0
            for t in range(LAGS):
                if not t & k:
                    x, y = pieces[t], pieces[t | k]
                    pieces[t] = jnp.where(low, x, pltpu.roll(y, k, 1))
                    pieces[t | k] = jnp.where(low, pltpu.roll(x, LANES - k, 1), y)
        for b in range(LAGS):
            dec_ref[r : r + 16, b * LANES : (b + 1) * LANES] = pieces[b]


def pick_kernel(dec_ref, ids, refch, keep_ref, give_ref):
    rows = dec_ref.shape[0]
    count = keep_ref.shape[0]
    core = lax.axis_index("core")
    own = lax.axis_index(AXES)
    at = own * rows
    line0 = at // LANES
    line1 = jnp.minimum(line0 + 1, ids.shape[0] - 1)
    turn = LANES - (at - line0 * LANES)
    pair = [
        pltpu.roll(jnp.broadcast_to(ids[pl.ds(i, 1), :], (8, LANES)), turn, 1) for i in (line0, line1)
    ]
    mine = jnp.where(iota((8, LANES), 1) < turn, pair[0], pair[1])[0:1, :rows]
    refcol = jnp.transpose(jnp.broadcast_to(refch[...], (LANES, NREF)))[:, :rows]
    select = jnp.where(refcol == mine, 1.0, 0.0)
    halves = (select[:count], select[count:])
    halves = (jnp.where(core == 0, *halves), jnp.where(core == 0, *halves[::-1]))
    select = jnp.concatenate(halves, axis=0).astype(BF16)
    for b in range(0, LAGS, 2):
        span = slice(b * LANES, (b + 2) * LANES)
        picked = jnp.dot(select, dec_ref[:, span], preferred_element_type=F32).astype(BF16)
        keep_ref[:, span] = picked[:count]
        give_ref[:, span] = picked[count:]


def route_kernel(dec_ref, owner_ref, packet_ref, stage):
    rows = owner_ref.shape[1]
    owner = owner_ref[...]
    chip = iota((CHIPS, rows), 0)
    before = (iota((rows, rows), 0) < iota((rows, rows), 1)).astype(BF16)
    parts = []
    for core in range(2):
        device = (chip // 4) * 8 + core * 4 + chip % 4
        one = jnp.where(device == owner, 1.0, 0.0)
        rank = jnp.dot(one.astype(BF16), before, preferred_element_type=F32)
        first = jnp.where(rank < 0.5, one, 0.0)
        parts += [first, one - first]
    select = jnp.concatenate(parts, axis=0).astype(BF16)
    for b in range(0, LAGS, 2):
        picked = jnp.dot(select, dec_ref[:, b * LANES : (b + 2) * LANES], preferred_element_type=F32)
        for g in range(4):
            for h in range(2):
                stage[pl.ds(g * LAGS + b + h, CHIPS, stride=4 * LAGS + PAD), :] = picked[
                    g * CHIPS : (g + 1) * CHIPS, h * LANES : (h + 1) * LANES
                ]
    for g in range(CHIPS):
        at = g * (4 * LAGS + PAD)
        packet_ref[g, : 4 * LAGS, :] = stage[at : at + 4 * LAGS, :].astype(BF16)


def add_refs_kernel(packet_in, keep_ref, got_ref, packet_ref, stage):
    del packet_in
    for s in range(2):
        rows = slice(s * CHIPS, (s + 1) * CHIPS)
        for b in range(LAGS):
            lanes = slice(b * LANES, (b + 1) * LANES)
            stage[pl.ds(s * LAGS + b, CHIPS, stride=2 * LAGS + PAD), :] = keep_ref[rows, lanes].astype(F32) + got_ref[
                rows, lanes
            ].astype(F32)
    for g in range(CHIPS):
        at = g * (2 * LAGS + PAD)
        packet_ref[g, 4 * LAGS :, :] = stage[at : at + 2 * LAGS, :].astype(BF16)


def spread_kernel(arrived_ref, spread_ref, give_ref):
    core = lax.axis_index("core")
    total = jnp.sum(arrived_ref[:, 4 * LAGS :, :].astype(F32), axis=0, keepdims=True)
    spread_ref[...] = jnp.broadcast_to(total, spread_ref.shape).astype(BF16)
    other = pl.multiple_of((1 - core) * 2 * LAGS, 2 * LAGS)
    give_ref[...] = arrived_ref[:, pl.ds(other, 2 * LAGS), :]


def lay_out_refs(refs_ref, wide, write):
    for g in range(CHIPS):
        at = g * (2 * LAGS + PAD)
        wide[at : at + 2 * LAGS, :] = refs_ref[g].astype(F32)
    for s in range(2):
        for b in range(LAGS):
            write(s * CHIPS, b * LANES, wide[pl.ds(s * LAGS + b, CHIPS, stride=2 * LAGS + PAD), :].astype(BF16))


def widen_kernel(arrived_ref, got_ref, own_ref, ext_ref, mine_ref, wide, wide_refs):
    core = lax.axis_index("core")
    mine = pl.multiple_of(core * 2 * LAGS, 2 * LAGS)
    for g in range(CHIPS):
        for slot in range(2):
            at = (2 * g + slot) * (LAGS + PAD)
            wide[core, at : at + LAGS, :] = arrived_ref[g, pl.ds(mine + slot * LAGS, LAGS), :].astype(F32)
            wide[1 - core, at : at + LAGS, :] = got_ref[g, slot * LAGS : (slot + 1) * LAGS, :].astype(F32)
    total = LAGS * LANES
    lane = iota((4 * CHIPS, LANES), 1)
    for b in range(LAGS):
        halves = [wide[c, pl.ds(b, 2 * CHIPS, stride=LAGS + PAD), :].reshape(CHIPS // 4, 1, 8, LANES) for c in range(2)]
        plane = jnp.concatenate(halves, axis=1).reshape(4 * CHIPS, LANES)
        ext_ref[:, b * LANES : (b + 1) * LANES] = plane.astype(BF16)
        moved = jnp.where(
            lane < LANES - LAGS, pltpu.roll(plane, LANES - LAGS, 1), pltpu.roll(plane, LANES - LAGS - 1, 1)
        )
        moved = jnp.where(lane == LANES - 1, 0.0, moved)
        ext_ref[:, total + b * LANES : total + (b + 1) * LANES] = moved.astype(BF16)

    def write(row, lane, piece):
        mine_ref[row : row + CHIPS, lane : lane + LANES] = piece

    lay_out_refs(own_ref, wide_refs, write)


def correlate_kernel(ext_ref, mine_ref, other_ref, out_hbm, wide, refs, sums, sem):
    total = LAGS * LANES
    core = lax.axis_index("core")
    half = NREF // 2

    def write(row, lane, piece):
        row = pl.multiple_of((1 - core) * half + row, CHIPS)
        refs[pl.ds(row, CHIPS), lane : lane + LANES] = piece

    refs[pl.ds(pl.multiple_of(core * half, half), half), :] = mine_ref[...]
    lay_out_refs(other_ref, wide, write)
    rows = ext_ref.shape[0]
    copies = []
    lag = 1
    for step, per in enumerate(LAG_STEPS):
        windows = [ext_ref[:, pl.ds((lag + i) * LANES, total)] for i in range(per)]
        part = dot_nt(jnp.concatenate(windows, axis=0), refs[...]) * (1.0 / math.sqrt(total))
        for i in range(per):
            sums[:, (lag - 1 + i) * NREF : (lag + i) * NREF] = part[i * rows : (i + 1) * rows]
        span = pl.ds((lag - 1) * NREF, per * NREF)
        copies.append(pltpu.make_async_copy(sums.at[:, span], out_hbm.at[0, :, span], sem.at[step]))
        copies[-1].start()
        lag += per
    for copy in copies:
        copy.wait()


def swap_cores(x):
    return lax.ppermute(x, "core", [(0, 1), (1, 0)])


def on_device(raw, taps, row_channel, ref_channel, owner_of_row):
    rows_dev, samples = raw.shape
    total = samples // STRIDE
    window = BLOCK * STRIDE + 2 * HALO
    half = jax.ShapeDtypeStruct((CHIPS, 2 * LAGS, LANES), BF16)
    plain = jax.ShapeDtypeStruct((NREF // 2, total), BF16)
    ids = row_channel.reshape(-1, LANES)
    dec = pl.pallas_call(
        decimate_kernel,
        out_shape=jax.ShapeDtypeStruct((rows_dev, total), BF16),
        in_specs=[HBM, VMEM],
        out_specs=VMEM,
        scratch_shapes=[
            pltpu.VMEM((rows_dev, samples + 2 * HALO), BF16),
            pltpu.VMEM((8, 3 * LANES), F32),
            pltpu.VMEM((BLOCK, window), BF16),
            pltpu.VMEM((rows_dev, total), BF16),
            pltpu.SemaphoreType.DMA,
        ],
        compiler_params=params(52),
        name="decimate",
    )(raw, taps.reshape(1, TAPS))
    keep, give = pl.pallas_call(
        pick_kernel,
        out_shape=(plain, plain),
        in_specs=[VMEM] * 3,
        out_specs=(VMEM, VMEM),
        compiler_params=params(),
        name="pick",
    )(dec, ids, ref_channel.reshape(1, NREF))
    got = swap_cores(give)
    packet_shape = jax.ShapeDtypeStruct((CHIPS, 6 * LAGS, LANES), BF16)
    packet = pl.pallas_call(
        route_kernel,
        out_shape=packet_shape,
        in_specs=[VMEM, VMEM],
        out_specs=VMEM,
        scratch_shapes=[pltpu.VMEM((CHIPS * (4 * LAGS + PAD), LANES), F32)],
        compiler_params=params(),
        cost_estimate=pl.CostEstimate(flops=100_000_000, bytes_accessed=4_000_000, transcendentals=0),
        name="route",
    )(dec, owner_of_row.reshape(1, rows_dev))
    packet = pl.pallas_call(
        add_refs_kernel,
        out_shape=packet_shape,
        in_specs=[VMEM] * 3,
        out_specs=VMEM,
        scratch_shapes=[pltpu.VMEM((CHIPS * (2 * LAGS + PAD), LANES), F32)],
        input_output_aliases={0: 0},
        compiler_params=params(),
        name="add_refs",
    )(packet, keep, got)
    arrived = lax.all_to_all(packet, SAME, 0, 0, tiled=True)
    spread, rows_give = pl.pallas_call(
        spread_kernel,
        out_shape=(half, half),
        in_specs=[VMEM],
        out_specs=(VMEM, VMEM),
        compiler_params=params(),
        name="spread",
    )(arrived)
    refs_own = lax.all_to_all(spread, SAME, 0, 0, tiled=True)
    rows_got = swap_cores(rows_give)
    ext, refs_mine = pl.pallas_call(
        widen_kernel,
        out_shape=(jax.ShapeDtypeStruct((4 * CHIPS, 2 * total), BF16), plain),
        in_specs=[VMEM, VMEM, VMEM],
        out_specs=(VMEM, VMEM),
        scratch_shapes=[
            pltpu.VMEM((2, CHIPS * 2 * (LAGS + PAD), LANES), F32),
            pltpu.VMEM((CHIPS * (2 * LAGS + PAD), LANES), F32),
        ],
        compiler_params=params(),
        name="widen",
    )(arrived, rows_got, refs_own)
    refs_other = swap_cores(refs_own)
    return pl.pallas_call(
        correlate_kernel,
        out_shape=jax.ShapeDtypeStruct((1, 4 * CHIPS, LAGS * NREF), F32),
        in_specs=[VMEM, VMEM, VMEM],
        out_specs=HBM,
        scratch_shapes=[
            pltpu.VMEM((CHIPS * (2 * LAGS + PAD), LANES), F32),
            pltpu.VMEM((NREF, total), BF16),
            pltpu.VMEM((4 * CHIPS, LAGS * NREF), F32),
            pltpu.SemaphoreType.DMA((len(LAG_STEPS),)),
        ],
        compiler_params=params(24),
        name="correlate",
    )(ext, refs_mine, refs_other)


def solution(mesh):
    parts = Mesh(mesh.devices.reshape(4, 4, 2, 4), AXES)
    return jax.shard_map(
        on_device,
        mesh=parts,
        in_specs=(P(AXES, None), P(), P(), P(), P(AXES, None)),
        out_specs=P(AXES, None, None),
        check_vma=False,
    )
```

```python
import math

import jax
import jax.numpy as jnp
from jax import lax
from jax.experimental import pallas as pl
from jax.experimental.pallas import tpu as pltpu
from jax.sharding import Mesh
from jax.sharding import PartitionSpec as P

LAGS = 16
TAPS = 127
STRIDE = 8
NREF = 256
LANES = 128
BLOCK = 128
HALO = 128
CHIPS = 64
PAD = 8
LAG_STEPS = (3, 5, 4, 2, 2)
AXES = ("x", "z", "core", "chan")
SAME = ("x", "z", "chan")
NT = (((1,), (1,)), ((), ()))
VMEM = pl.BlockSpec(memory_space=pltpu.VMEM)
HBM = pl.BlockSpec(memory_space=pltpu.HBM)
F32, BF16 = jnp.float32, jnp.bfloat16


def dot_nt(a, b):
    return lax.dot_general(a, b, NT, preferred_element_type=F32)


def params(mib=48):
    return pltpu.CompilerParams(vmem_limit_bytes=mib << 20)


def iota(shape, dim):
    return lax.broadcasted_iota(jnp.int32, shape, dim)


def decimate_kernel(raw_hbm, taps, dec_ref, raw, line, band, dec, sem):
    rows = dec_ref.shape[0]
    chunk = BLOCK * STRIDE
    window = chunk + 2 * HALO
    load = pltpu.make_async_copy(raw_hbm, raw.at[:, pl.ds(HALO, raw_hbm.shape[1])], sem)
    load.start()
    raw[:, :HALO] = jnp.zeros((rows, HALO), BF16)
    raw[:, raw.shape[1] - HALO :] = jnp.zeros((rows, HALO), BF16)
    line[...] = jnp.zeros_like(line)
    band[...] = jnp.zeros_like(band)
    line[0:1, 0:TAPS] = taps[...].astype(F32)
    width = line.shape[1]
    first = pltpu.roll(
        jnp.broadcast_to(line[0:1, :], (16, width)), HALO - TAPS // 2, 1, stride=STRIDE, stride_axis=0
    ).astype(BF16)
    for i in range(BLOCK // 16):
        band[16 * i : 16 * (i + 1), LANES * i : LANES * i + width] = first
    load.wait()
    for at in range(0, LAGS, 2):
        windows = [raw[:, pl.ds((at + i) * chunk, window)] for i in range(2)]
        part = dot_nt(jnp.concatenate(windows, axis=0), band[...])
        for i in range(2):
            dec[:, (at + i) * LANES : (at + i + 1) * LANES] = part[i * rows : (i + 1) * rows].astype(BF16)
    lane = iota((16, LANES), 1)
    for r in range(0, rows, 16):
        pieces = [dec[r : r + 16, m * LANES : (m + 1) * LANES] for m in range(LAGS)]
        for k in (1, 2, 4, 8):
            low = (lane & k) == 0
            for t in range(LAGS):
                if not t & k:
                    x, y = pieces[t], pieces[t | k]
                    pieces[t] = jnp.where(low, x, pltpu.roll(y, k, 1))
                    pieces[t | k] = jnp.where(low, pltpu.roll(x, LANES - k, 1), y)
        for b in range(LAGS):
            dec_ref[r : r + 16, b * LANES : (b + 1) * LANES] = pieces[b]


def find_kernel(ids, refch, select_ref):
    count, rows = select_ref.shape[1:]
    core = lax.axis_index("core")
    own = lax.axis_index(AXES)
    refcol = jnp.transpose(jnp.broadcast_to(refch[...], (LANES, NREF)))[:, :rows]
    refcol = jnp.where(core == 0, refcol[:count], refcol[count:])
    for i, device in enumerate((own, own + 4 - 8 * core)):
        at = device * rows
        line0 = at // LANES
        line1 = jnp.minimum(line0 + 1, ids.shape[0] - 1)
        turn = LANES - (at - line0 * LANES)
        pair = [
            pltpu.roll(jnp.broadcast_to(ids[pl.ds(k, 1), :], (8, LANES)), turn, 1) for k in (line0, line1)
        ]
        there = jnp.where(iota((8, LANES), 1) < turn, pair[0], pair[1])[0:1, :rows]
        select_ref[i] = jnp.where(refcol == there, 1.0, 0.0).astype(BF16)


def route_kernel(dec_ref, owner_ref, packet_ref, stage):
    rows = owner_ref.shape[1]
    owner = owner_ref[...]
    chip = iota((CHIPS, rows), 0)
    before = (iota((rows, rows), 0) < iota((rows, rows), 1)).astype(BF16)
    parts = []
    for core in range(2):
        device = (chip // 4) * 8 + core * 4 + chip % 4
        one = jnp.where(device == owner, 1.0, 0.0)
        rank = jnp.dot(one.astype(BF16), before, preferred_element_type=F32)
        first = jnp.where(rank < 0.5, one, 0.0)
        parts += [first, one - first]
    select = jnp.concatenate(parts, axis=0).astype(BF16)
    for b in range(0, LAGS, 2):
        picked = jnp.dot(select, dec_ref[:, b * LANES : (b + 2) * LANES], preferred_element_type=F32)
        for g in range(4):
            for h in range(2):
                stage[pl.ds(g * LAGS + b + h, CHIPS, stride=4 * LAGS + PAD), :] = picked[
                    g * CHIPS : (g + 1) * CHIPS, h * LANES : (h + 1) * LANES
                ]
    for g in range(CHIPS):
        at = g * (4 * LAGS + PAD)
        packet_ref[g, : 4 * LAGS, :] = stage[at : at + 4 * LAGS, :].astype(BF16)


def add_refs_kernel(packet_in, select_ref, dec_ref, got_ref, packet_ref, stage):
    del packet_in
    for b in range(0, LAGS, 2):
        span = slice(b * LANES, (b + 2) * LANES)
        picked = jnp.dot(select_ref[0], dec_ref[:, span], preferred_element_type=F32)
        picked = picked + jnp.dot(select_ref[1], got_ref[:, span], preferred_element_type=F32)
        for s in range(2):
            for h in range(2):
                stage[pl.ds(s * LAGS + b + h, CHIPS, stride=2 * LAGS + PAD), :] = picked[
                    s * CHIPS : (s + 1) * CHIPS, h * LANES : (h + 1) * LANES
                ]
    for g in range(CHIPS):
        at = g * (2 * LAGS + PAD)
        packet_ref[g, 4 * LAGS :, :] = stage[at : at + 2 * LAGS, :].astype(BF16)


def spread_kernel(arrived_ref, spread_ref, give_ref):
    core = lax.axis_index("core")
    total = jnp.sum(arrived_ref[:, 4 * LAGS :, :].astype(F32), axis=0, keepdims=True)
    spread_ref[...] = jnp.broadcast_to(total, spread_ref.shape).astype(BF16)
    other = pl.multiple_of((1 - core) * 2 * LAGS, 2 * LAGS)
    give_ref[...] = arrived_ref[:, pl.ds(other, 2 * LAGS), :]


def lay_out_refs(refs_ref, wide, write):
    for g in range(CHIPS):
        at = g * (2 * LAGS + PAD)
        wide[at : at + 2 * LAGS, :] = refs_ref[g].astype(F32)
    for s in range(2):
        for b in range(LAGS):
            write(s * CHIPS, b * LANES, wide[pl.ds(s * LAGS + b, CHIPS, stride=2 * LAGS + PAD), :].astype(BF16))


def widen_kernel(arrived_ref, got_ref, own_ref, ext_ref, mine_ref, wide, wide_refs):
    core = lax.axis_index("core")
    mine = pl.multiple_of(core * 2 * LAGS, 2 * LAGS)
    for g in range(CHIPS):
        for slot in range(2):
            at = (2 * g + slot) * (LAGS + PAD)
            wide[core, at : at + LAGS, :] = arrived_ref[g, pl.ds(mine + slot * LAGS, LAGS), :].astype(F32)
            wide[1 - core, at : at + LAGS, :] = got_ref[g, slot * LAGS : (slot + 1) * LAGS, :].astype(F32)
    total = LAGS * LANES
    lane = iota((4 * CHIPS, LANES), 1)
    for b in range(LAGS):
        halves = [wide[c, pl.ds(b, 2 * CHIPS, stride=LAGS + PAD), :].reshape(CHIPS // 4, 1, 8, LANES) for c in range(2)]
        plane = jnp.concatenate(halves, axis=1).reshape(4 * CHIPS, LANES)
        ext_ref[:, b * LANES : (b + 1) * LANES] = plane.astype(BF16)
        moved = jnp.where(
            lane < LANES - LAGS, pltpu.roll(plane, LANES - LAGS, 1), pltpu.roll(plane, LANES - LAGS - 1, 1)
        )
        moved = jnp.where(lane == LANES - 1, 0.0, moved)
        ext_ref[:, total + b * LANES : total + (b + 1) * LANES] = moved.astype(BF16)

    def write(row, lane, piece):
        mine_ref[row : row + CHIPS, lane : lane + LANES] = piece

    lay_out_refs(own_ref, wide_refs, write)


def correlate_kernel(ext_ref, mine_ref, other_ref, out_hbm, wide, refs, sums, sem):
    total = LAGS * LANES
    core = lax.axis_index("core")
    half = NREF // 2

    def write(row, lane, piece):
        row = pl.multiple_of((1 - core) * half + row, CHIPS)
        refs[pl.ds(row, CHIPS), lane : lane + LANES] = piece

    refs[pl.ds(pl.multiple_of(core * half, half), half), :] = mine_ref[...]
    lay_out_refs(other_ref, wide, write)
    rows = ext_ref.shape[0]
    copies = []
    lag = 1
    for step, per in enumerate(LAG_STEPS):
        windows = [ext_ref[:, pl.ds((lag + i) * LANES, total)] for i in range(per)]
        part = dot_nt(jnp.concatenate(windows, axis=0), refs[...]) * (1.0 / math.sqrt(total))
        for i in range(per):
            sums[:, (lag - 1 + i) * NREF : (lag + i) * NREF] = part[i * rows : (i + 1) * rows]
        span = pl.ds((lag - 1) * NREF, per * NREF)
        copies.append(pltpu.make_async_copy(sums.at[:, span], out_hbm.at[0, :, span], sem.at[step]))
        copies[-1].start()
        lag += per
    for copy in copies:
        copy.wait()


def swap_cores(x):
    return lax.ppermute(x, "core", [(0, 1), (1, 0)])


def on_device(raw, taps, row_channel, ref_channel, owner_of_row):
    rows_dev, samples = raw.shape
    total = samples // STRIDE
    window = BLOCK * STRIDE + 2 * HALO
    half = jax.ShapeDtypeStruct((CHIPS, 2 * LAGS, LANES), BF16)
    plain = jax.ShapeDtypeStruct((NREF // 2, total), BF16)
    ids = row_channel.reshape(-1, LANES)
    dec = pl.pallas_call(
        decimate_kernel,
        out_shape=jax.ShapeDtypeStruct((rows_dev, total), BF16),
        in_specs=[HBM, VMEM],
        out_specs=VMEM,
        scratch_shapes=[
            pltpu.VMEM((rows_dev, samples + 2 * HALO), BF16),
            pltpu.VMEM((8, 3 * LANES), F32),
            pltpu.VMEM((BLOCK, window), BF16),
            pltpu.VMEM((rows_dev, total), BF16),
            pltpu.SemaphoreType.DMA,
        ],
        compiler_params=params(52),
        name="decimate",
    )(raw, taps.reshape(1, TAPS))
    got = swap_cores(dec)
    select = pl.pallas_call(
        find_kernel,
        out_shape=jax.ShapeDtypeStruct((2, NREF // 2, rows_dev), BF16),
        in_specs=[VMEM] * 2,
        out_specs=VMEM,
        compiler_params=params(),
        name="find",
    )(ids, ref_channel.reshape(1, NREF))
    packet_shape = jax.ShapeDtypeStruct((CHIPS, 6 * LAGS, LANES), BF16)
    packet = pl.pallas_call(
        route_kernel,
        out_shape=packet_shape,
        in_specs=[VMEM, VMEM],
        out_specs=VMEM,
        scratch_shapes=[pltpu.VMEM((CHIPS * (4 * LAGS + PAD), LANES), F32)],
        compiler_params=params(),
        cost_estimate=pl.CostEstimate(flops=100_000_000, bytes_accessed=4_000_000, transcendentals=0),
        name="route",
    )(dec, owner_of_row.reshape(1, rows_dev))
    packet = pl.pallas_call(
        add_refs_kernel,
        out_shape=packet_shape,
        in_specs=[VMEM] * 4,
        out_specs=VMEM,
        scratch_shapes=[pltpu.VMEM((CHIPS * (2 * LAGS + PAD), LANES), F32)],
        input_output_aliases={0: 0},
        compiler_params=params(),
        name="add_refs",
    )(packet, select, dec, got)
    arrived = lax.all_to_all(packet, SAME, 0, 0, tiled=True)
    spread, rows_give = pl.pallas_call(
        spread_kernel,
        out_shape=(half, half),
        in_specs=[VMEM],
        out_specs=(VMEM, VMEM),
        compiler_params=params(),
        name="spread",
    )(arrived)
    refs_own = lax.all_to_all(spread, SAME, 0, 0, tiled=True)
    rows_got = swap_cores(rows_give)
    ext, refs_mine = pl.pallas_call(
        widen_kernel,
        out_shape=(jax.ShapeDtypeStruct((4 * CHIPS, 2 * total), BF16), plain),
        in_specs=[VMEM, VMEM, VMEM],
        out_specs=(VMEM, VMEM),
        scratch_shapes=[
            pltpu.VMEM((2, CHIPS * 2 * (LAGS + PAD), LANES), F32),
            pltpu.VMEM((CHIPS * (2 * LAGS + PAD), LANES), F32),
        ],
        compiler_params=params(),
        name="widen",
    )(arrived, rows_got, refs_own)
    refs_other = swap_cores(refs_own)
    return pl.pallas_call(
        correlate_kernel,
        out_shape=jax.ShapeDtypeStruct((1, 4 * CHIPS, LAGS * NREF), F32),
        in_specs=[VMEM, VMEM, VMEM],
        out_specs=HBM,
        scratch_shapes=[
            pltpu.VMEM((CHIPS * (2 * LAGS + PAD), LANES), F32),
            pltpu.VMEM((NREF, total), BF16),
            pltpu.VMEM((4 * CHIPS, LAGS * NREF), F32),
            pltpu.SemaphoreType.DMA((len(LAG_STEPS),)),
        ],
        compiler_params=params(24),
        name="correlate",
    )(ext, refs_mine, refs_other)


def solution(mesh):
    parts = Mesh(mesh.devices.reshape(4, 4, 2, 4), AXES)
    return jax.shard_map(
        on_device,
        mesh=parts,
        in_specs=(P(AXES, None), P(), P(), P(), P(AXES, None)),
        out_specs=P(AXES, None, None),
        check_vma=False,
    )
```

```python
import math

import jax
import jax.numpy as jnp
from jax import lax
from jax.experimental import pallas as pl
from jax.experimental.pallas import tpu as pltpu
from jax.sharding import Mesh
from jax.sharding import PartitionSpec as P

LAGS = 16
TAPS = 127
STRIDE = 8
NREF = 256
LANES = 128
BLOCK = 128
HALO = 128
CHIPS = 64
PAD = 8
LAG_STEPS = (3, 5, 4, 2, 2)
AXES = ("x", "z", "core", "chan")
SAME = ("x", "z", "chan")
NT = (((1,), (1,)), ((), ()))
VMEM = pl.BlockSpec(memory_space=pltpu.VMEM)
HBM = pl.BlockSpec(memory_space=pltpu.HBM)
F32, BF16 = jnp.float32, jnp.bfloat16


def dot_nt(a, b):
    return lax.dot_general(a, b, NT, preferred_element_type=F32)


def params(mib=48):
    return pltpu.CompilerParams(vmem_limit_bytes=mib << 20)


def iota(shape, dim):
    return lax.broadcasted_iota(jnp.int32, shape, dim)


def decimate_kernel(raw_hbm, taps, dec_ref, raw, line, band, dec, sem):
    rows = dec_ref.shape[0]
    chunk = BLOCK * STRIDE
    window = chunk + 2 * HALO
    load = pltpu.make_async_copy(raw_hbm, raw.at[:, pl.ds(HALO, raw_hbm.shape[1])], sem)
    load.start()
    raw[:, :HALO] = jnp.zeros((rows, HALO), BF16)
    raw[:, raw.shape[1] - HALO :] = jnp.zeros((rows, HALO), BF16)
    line[...] = jnp.zeros_like(line)
    band[...] = jnp.zeros_like(band)
    line[0:1, 0:TAPS] = taps[...].astype(F32)
    width = line.shape[1]
    first = pltpu.roll(
        jnp.broadcast_to(line[0:1, :], (16, width)), HALO - TAPS // 2, 1, stride=STRIDE, stride_axis=0
    ).astype(BF16)
    for i in range(BLOCK // 16):
        band[16 * i : 16 * (i + 1), LANES * i : LANES * i + width] = first
    load.wait()
    for at in range(0, LAGS, 2):
        windows = [raw[:, pl.ds((at + i) * chunk, window)] for i in range(2)]
        part = dot_nt(jnp.concatenate(windows, axis=0), band[...])
        for i in range(2):
            dec[:, (at + i) * LANES : (at + i + 1) * LANES] = part[i * rows : (i + 1) * rows].astype(BF16)
    lane = iota((16, LANES), 1)
    for r in range(0, rows, 16):
        pieces = [dec[r : r + 16, m * LANES : (m + 1) * LANES] for m in range(LAGS)]
        for k in (1, 2, 4, 8):
            low = (lane & k) == 0
            for t in range(LAGS):
                if not t & k:
                    x, y = pieces[t], pieces[t | k]
                    pieces[t] = jnp.where(low, x, pltpu.roll(y, k, 1))
                    pieces[t | k] = jnp.where(low, pltpu.roll(x, LANES - k, 1), y)
        for b in range(LAGS):
            dec_ref[r : r + 16, b * LANES : (b + 1) * LANES] = pieces[b]


def find_kernel(ids, refch, dec_ref, select_ref, keep_ref):
    count, rows = select_ref.shape
    core = lax.axis_index("core")
    own = lax.axis_index(AXES)
    refcol = jnp.transpose(jnp.broadcast_to(refch[...], (LANES, NREF)))[:, :rows]
    refcol = jnp.where(core == 0, refcol[:count], refcol[count:])
    for i, device in enumerate((own, own + 4 - 8 * core)):
        at = device * rows
        line0 = at // LANES
        line1 = jnp.minimum(line0 + 1, ids.shape[0] - 1)
        turn = LANES - (at - line0 * LANES)
        pair = [
            pltpu.roll(jnp.broadcast_to(ids[pl.ds(k, 1), :], (8, LANES)), turn, 1) for k in (line0, line1)
        ]
        there = jnp.where(iota((8, LANES), 1) < turn, pair[0], pair[1])[0:1, :rows]
        select = jnp.where(refcol == there, 1.0, 0.0).astype(BF16)
        if i:
            select_ref[...] = select
        else:
            keep_ref[...] = jnp.dot(select, dec_ref[...], preferred_element_type=F32).astype(BF16)


def route_kernel(dec_ref, owner_ref, packet_ref, stage):
    rows = owner_ref.shape[1]
    owner = owner_ref[...]
    chip = iota((CHIPS, rows), 0)
    before = (iota((rows, rows), 0) < iota((rows, rows), 1)).astype(BF16)
    parts = []
    for core in range(2):
        device = (chip // 4) * 8 + core * 4 + chip % 4
        one = jnp.where(device == owner, 1.0, 0.0)
        rank = jnp.dot(one.astype(BF16), before, preferred_element_type=F32)
        first = jnp.where(rank < 0.5, one, 0.0)
        parts += [first, one - first]
    select = jnp.concatenate(parts, axis=0).astype(BF16)
    for b in range(0, LAGS, 2):
        picked = jnp.dot(select, dec_ref[:, b * LANES : (b + 2) * LANES], preferred_element_type=F32)
        for g in range(4):
            for h in range(2):
                stage[pl.ds(g * LAGS + b + h, CHIPS, stride=4 * LAGS + PAD), :] = picked[
                    g * CHIPS : (g + 1) * CHIPS, h * LANES : (h + 1) * LANES
                ]
    for g in range(CHIPS):
        at = g * (4 * LAGS + PAD)
        packet_ref[g, : 4 * LAGS, :] = stage[at : at + 4 * LAGS, :].astype(BF16)


def add_refs_kernel(packet_in, select_ref, keep_ref, got_ref, packet_ref, stage):
    del packet_in
    for b in range(0, LAGS, 2):
        span = slice(b * LANES, (b + 2) * LANES)
        picked = jnp.dot(select_ref[...], got_ref[:, span], preferred_element_type=F32)
        picked = picked + keep_ref[:, span].astype(F32)
        for s in range(2):
            for h in range(2):
                stage[pl.ds(s * LAGS + b + h, CHIPS, stride=2 * LAGS + PAD), :] = picked[
                    s * CHIPS : (s + 1) * CHIPS, h * LANES : (h + 1) * LANES
                ]
    for g in range(CHIPS):
        at = g * (2 * LAGS + PAD)
        packet_ref[g, 4 * LAGS :, :] = stage[at : at + 2 * LAGS, :].astype(BF16)


def spread_kernel(arrived_ref, spread_ref, give_ref):
    core = lax.axis_index("core")
    total = jnp.sum(arrived_ref[:, 4 * LAGS :, :].astype(F32), axis=0, keepdims=True)
    spread_ref[...] = jnp.broadcast_to(total, spread_ref.shape).astype(BF16)
    other = pl.multiple_of((1 - core) * 2 * LAGS, 2 * LAGS)
    give_ref[...] = arrived_ref[:, pl.ds(other, 2 * LAGS), :]


def lay_out_refs(refs_ref, wide, write):
    for g in range(CHIPS):
        at = g * (2 * LAGS + PAD)
        wide[at : at + 2 * LAGS, :] = refs_ref[g].astype(F32)
    for s in range(2):
        for b in range(LAGS):
            write(s * CHIPS, b * LANES, wide[pl.ds(s * LAGS + b, CHIPS, stride=2 * LAGS + PAD), :].astype(BF16))


def widen_kernel(arrived_ref, got_ref, own_ref, ext_ref, mine_ref, wide, wide_refs):
    core = lax.axis_index("core")
    mine = pl.multiple_of(core * 2 * LAGS, 2 * LAGS)
    for g in range(CHIPS):
        for slot in range(2):
            at = (2 * g + slot) * (LAGS + PAD)
            wide[core, at : at + LAGS, :] = arrived_ref[g, pl.ds(mine + slot * LAGS, LAGS), :].astype(F32)
            wide[1 - core, at : at + LAGS, :] = got_ref[g, slot * LAGS : (slot + 1) * LAGS, :].astype(F32)
    total = LAGS * LANES
    lane = iota((4 * CHIPS, LANES), 1)
    for b in range(LAGS):
        halves = [wide[c, pl.ds(b, 2 * CHIPS, stride=LAGS + PAD), :].reshape(CHIPS // 4, 1, 8, LANES) for c in range(2)]
        plane = jnp.concatenate(halves, axis=1).reshape(4 * CHIPS, LANES)
        ext_ref[:, b * LANES : (b + 1) * LANES] = plane.astype(BF16)
        moved = jnp.where(
            lane < LANES - LAGS, pltpu.roll(plane, LANES - LAGS, 1), pltpu.roll(plane, LANES - LAGS - 1, 1)
        )
        moved = jnp.where(lane == LANES - 1, 0.0, moved)
        ext_ref[:, total + b * LANES : total + (b + 1) * LANES] = moved.astype(BF16)

    def write(row, lane, piece):
        mine_ref[row : row + CHIPS, lane : lane + LANES] = piece

    lay_out_refs(own_ref, wide_refs, write)


def correlate_kernel(ext_ref, mine_ref, other_ref, out_hbm, wide, refs, sums, sem):
    total = LAGS * LANES
    core = lax.axis_index("core")
    half = NREF // 2

    def write(row, lane, piece):
        row = pl.multiple_of((1 - core) * half + row, CHIPS)
        refs[pl.ds(row, CHIPS), lane : lane + LANES] = piece

    refs[pl.ds(pl.multiple_of(core * half, half), half), :] = mine_ref[...]
    lay_out_refs(other_ref, wide, write)
    rows = ext_ref.shape[0]
    copies = []
    lag = 1
    for step, per in enumerate(LAG_STEPS):
        windows = [ext_ref[:, pl.ds((lag + i) * LANES, total)] for i in range(per)]
        part = dot_nt(jnp.concatenate(windows, axis=0), refs[...]) * (1.0 / math.sqrt(total))
        for i in range(per):
            sums[:, (lag - 1 + i) * NREF : (lag + i) * NREF] = part[i * rows : (i + 1) * rows]
        span = pl.ds((lag - 1) * NREF, per * NREF)
        copies.append(pltpu.make_async_copy(sums.at[:, span], out_hbm.at[0, :, span], sem.at[step]))
        copies[-1].start()
        lag += per
    for copy in copies:
        copy.wait()


def swap_cores(x):
    return lax.ppermute(x, "core", [(0, 1), (1, 0)])


def on_device(raw, taps, row_channel, ref_channel, owner_of_row):
    rows_dev, samples = raw.shape
    total = samples // STRIDE
    window = BLOCK * STRIDE + 2 * HALO
    half = jax.ShapeDtypeStruct((CHIPS, 2 * LAGS, LANES), BF16)
    plain = jax.ShapeDtypeStruct((NREF // 2, total), BF16)
    ids = row_channel.reshape(-1, LANES)
    dec = pl.pallas_call(
        decimate_kernel,
        out_shape=jax.ShapeDtypeStruct((rows_dev, total), BF16),
        in_specs=[HBM, VMEM],
        out_specs=VMEM,
        scratch_shapes=[
            pltpu.VMEM((rows_dev, samples + 2 * HALO), BF16),
            pltpu.VMEM((8, 3 * LANES), F32),
            pltpu.VMEM((BLOCK, window), BF16),
            pltpu.VMEM((rows_dev, total), BF16),
            pltpu.SemaphoreType.DMA,
        ],
        compiler_params=params(52),
        name="decimate",
    )(raw, taps.reshape(1, TAPS))
    got = swap_cores(dec)
    select, keep = pl.pallas_call(
        find_kernel,
        out_shape=(jax.ShapeDtypeStruct((NREF // 2, rows_dev), BF16), plain),
        in_specs=[VMEM] * 3,
        out_specs=(VMEM, VMEM),
        compiler_params=params(),
        name="find",
    )(ids, ref_channel.reshape(1, NREF), dec)
    packet_shape = jax.ShapeDtypeStruct((CHIPS, 6 * LAGS, LANES), BF16)
    packet = pl.pallas_call(
        route_kernel,
        out_shape=packet_shape,
        in_specs=[VMEM, VMEM],
        out_specs=VMEM,
        scratch_shapes=[pltpu.VMEM((CHIPS * (4 * LAGS + PAD), LANES), F32)],
        compiler_params=params(),
        cost_estimate=pl.CostEstimate(flops=100_000_000, bytes_accessed=4_000_000, transcendentals=0),
        name="route",
    )(dec, owner_of_row.reshape(1, rows_dev))
    packet = pl.pallas_call(
        add_refs_kernel,
        out_shape=packet_shape,
        in_specs=[VMEM] * 4,
        out_specs=VMEM,
        scratch_shapes=[pltpu.VMEM((CHIPS * (2 * LAGS + PAD), LANES), F32)],
        input_output_aliases={0: 0},
        compiler_params=params(),
        name="add_refs",
    )(packet, select, keep, got)
    arrived = lax.all_to_all(packet, SAME, 0, 0, tiled=True)
    spread, rows_give = pl.pallas_call(
        spread_kernel,
        out_shape=(half, half),
        in_specs=[VMEM],
        out_specs=(VMEM, VMEM),
        compiler_params=params(),
        name="spread",
    )(arrived)
    refs_own = lax.all_to_all(spread, SAME, 0, 0, tiled=True)
    rows_got = swap_cores(rows_give)
    ext, refs_mine = pl.pallas_call(
        widen_kernel,
        out_shape=(jax.ShapeDtypeStruct((4 * CHIPS, 2 * total), BF16), plain),
        in_specs=[VMEM, VMEM, VMEM],
        out_specs=(VMEM, VMEM),
        scratch_shapes=[
            pltpu.VMEM((2, CHIPS * 2 * (LAGS + PAD), LANES), F32),
            pltpu.VMEM((CHIPS * (2 * LAGS + PAD), LANES), F32),
        ],
        compiler_params=params(),
        name="widen",
    )(arrived, rows_got, refs_own)
    refs_other = swap_cores(refs_own)
    return pl.pallas_call(
        correlate_kernel,
        out_shape=jax.ShapeDtypeStruct((1, 4 * CHIPS, LAGS * NREF), F32),
        in_specs=[VMEM, VMEM, VMEM],
        out_specs=HBM,
        scratch_shapes=[
            pltpu.VMEM((CHIPS * (2 * LAGS + PAD), LANES), F32),
            pltpu.VMEM((NREF, total), BF16),
            pltpu.VMEM((4 * CHIPS, LAGS * NREF), F32),
            pltpu.SemaphoreType.DMA((len(LAG_STEPS),)),
        ],
        compiler_params=params(24),
        name="correlate",
    )(ext, refs_mine, refs_other)


def solution(mesh):
    parts = Mesh(mesh.devices.reshape(4, 4, 2, 4), AXES)
    return jax.shard_map(
        on_device,
        mesh=parts,
        in_specs=(P(AXES, None), P(), P(), P(), P(AXES, None)),
        out_specs=P(AXES, None, None),
        check_vma=False,
    )
```

```python
import math

import jax
import jax.numpy as jnp
from jax import lax
from jax.experimental import pallas as pl
from jax.experimental.pallas import tpu as pltpu
from jax.sharding import Mesh
from jax.sharding import PartitionSpec as P

LAGS = 16
TAPS = 127
STRIDE = 8
NREF = 256
LANES = 128
BLOCK = 128
HALO = 128
CHIPS = 64
PAD = 8
LAG_STEPS = (3, 5, 4, 3, 1)
AXES = ("x", "z", "core", "chan")
SAME = ("x", "z", "chan")
NT = (((1,), (1,)), ((), ()))
VMEM = pl.BlockSpec(memory_space=pltpu.VMEM)
HBM = pl.BlockSpec(memory_space=pltpu.HBM)
F32, BF16 = jnp.float32, jnp.bfloat16


def dot_nt(a, b):
    return lax.dot_general(a, b, NT, preferred_element_type=F32)


def params(mib=48):
    return pltpu.CompilerParams(vmem_limit_bytes=mib << 20)


def iota(shape, dim):
    return lax.broadcasted_iota(jnp.int32, shape, dim)


def decimate_kernel(raw_hbm, taps, dec_ref, raw, line, band, dec, sem):
    rows = dec_ref.shape[0]
    chunk = BLOCK * STRIDE
    window = chunk + 2 * HALO
    load = pltpu.make_async_copy(raw_hbm, raw.at[:, pl.ds(HALO, raw_hbm.shape[1])], sem)
    load.start()
    raw[:, :HALO] = jnp.zeros((rows, HALO), BF16)
    raw[:, raw.shape[1] - HALO :] = jnp.zeros((rows, HALO), BF16)
    line[...] = jnp.zeros_like(line)
    band[...] = jnp.zeros_like(band)
    line[0:1, 0:TAPS] = taps[...].astype(F32)
    width = line.shape[1]
    first = pltpu.roll(
        jnp.broadcast_to(line[0:1, :], (16, width)), HALO - TAPS // 2, 1, stride=STRIDE, stride_axis=0
    ).astype(BF16)
    for i in range(BLOCK // 16):
        band[16 * i : 16 * (i + 1), LANES * i : LANES * i + width] = first
    load.wait()
    for at in range(0, LAGS, 2):
        windows = [raw[:, pl.ds((at + i) * chunk, window)] for i in range(2)]
        part = dot_nt(jnp.concatenate(windows, axis=0), band[...])
        for i in range(2):
            dec[:, (at + i) * LANES : (at + i + 1) * LANES] = part[i * rows : (i + 1) * rows].astype(BF16)
    lane = iota((16, LANES), 1)
    for r in range(0, rows, 16):
        pieces = [dec[r : r + 16, m * LANES : (m + 1) * LANES] for m in range(LAGS)]
        for k in (1, 2, 4, 8):
            low = (lane & k) == 0
            for t in range(LAGS):
                if not t & k:
                    x, y = pieces[t], pieces[t | k]
                    pieces[t] = jnp.where(low, x, pltpu.roll(y, k, 1))
                    pieces[t | k] = jnp.where(low, pltpu.roll(x, LANES - k, 1), y)
        for b in range(LAGS):
            dec_ref[r : r + 16, b * LANES : (b + 1) * LANES] = pieces[b]


def find_kernel(ids, refch, dec_ref, select_ref, keep_ref):
    count, rows = select_ref.shape
    core = lax.axis_index("core")
    own = lax.axis_index(AXES)
    refcol = jnp.transpose(jnp.broadcast_to(refch[...], (LANES, NREF)))[:, :rows]
    refcol = jnp.where(core == 0, refcol[:count], refcol[count:])
    for i, device in enumerate((own, own + 4 - 8 * core)):
        at = device * rows
        line0 = at // LANES
        line1 = jnp.minimum(line0 + 1, ids.shape[0] - 1)
        turn = LANES - (at - line0 * LANES)
        pair = [
            pltpu.roll(jnp.broadcast_to(ids[pl.ds(k, 1), :], (8, LANES)), turn, 1) for k in (line0, line1)
        ]
        there = jnp.where(iota((8, LANES), 1) < turn, pair[0], pair[1])[0:1, :rows]
        select = jnp.where(refcol == there, 1.0, 0.0).astype(BF16)
        if i:
            select_ref[...] = select
        else:
            keep_ref[...] = jnp.dot(select, dec_ref[...], preferred_element_type=F32).astype(BF16)


def route_kernel(dec_ref, owner_ref, packet_ref, stage):
    rows = owner_ref.shape[1]
    owner = owner_ref[...]
    chip = iota((CHIPS, rows), 0)
    before = (iota((rows, rows), 0) < iota((rows, rows), 1)).astype(BF16)
    parts = []
    for core in range(2):
        device = (chip // 4) * 8 + core * 4 + chip % 4
        one = jnp.where(device == owner, 1.0, 0.0)
        rank = jnp.dot(one.astype(BF16), before, preferred_element_type=F32)
        first = jnp.where(rank < 0.5, one, 0.0)
        parts += [first, one - first]
    select = jnp.concatenate(parts, axis=0).astype(BF16)
    for b in range(0, LAGS, 2):
        picked = jnp.dot(select, dec_ref[:, b * LANES : (b + 2) * LANES], preferred_element_type=F32)
        for g in range(4):
            for h in range(2):
                stage[pl.ds(g * LAGS + b + h, CHIPS, stride=4 * LAGS + PAD), :] = picked[
                    g * CHIPS : (g + 1) * CHIPS, h * LANES : (h + 1) * LANES
                ]
    for g in range(CHIPS):
        at = g * (4 * LAGS + PAD)
        packet_ref[g, : 4 * LAGS, :] = stage[at : at + 4 * LAGS, :].astype(BF16)


def add_refs_kernel(packet_in, select_ref, keep_ref, got_ref, packet_ref, stage):
    del packet_in
    for b in range(0, LAGS, 2):
        span = slice(b * LANES, (b + 2) * LANES)
        picked = jnp.dot(select_ref[...], got_ref[:, span], preferred_element_type=F32)
        picked = picked + keep_ref[:, span].astype(F32)
        for s in range(2):
            for h in range(2):
                stage[pl.ds(s * LAGS + b + h, CHIPS, stride=2 * LAGS + PAD), :] = picked[
                    s * CHIPS : (s + 1) * CHIPS, h * LANES : (h + 1) * LANES
                ]
    for g in range(CHIPS):
        at = g * (2 * LAGS + PAD)
        packet_ref[g, 4 * LAGS :, :] = stage[at : at + 2 * LAGS, :].astype(BF16)


def spread_kernel(arrived_ref, spread_ref, give_ref):
    core = lax.axis_index("core")
    total = jnp.sum(arrived_ref[:, 4 * LAGS :, :].astype(F32), axis=0, keepdims=True)
    spread_ref[...] = jnp.broadcast_to(total, spread_ref.shape).astype(BF16)
    other = pl.multiple_of((1 - core) * 2 * LAGS, 2 * LAGS)
    give_ref[...] = arrived_ref[:, pl.ds(other, 2 * LAGS), :]


def lay_out_refs(refs_ref, wide, write):
    for g in range(CHIPS):
        at = g * (2 * LAGS + PAD)
        wide[at : at + 2 * LAGS, :] = refs_ref[g].astype(F32)
    for s in range(2):
        for b in range(LAGS):
            write(s * CHIPS, b * LANES, wide[pl.ds(s * LAGS + b, CHIPS, stride=2 * LAGS + PAD), :].astype(BF16))


def widen_kernel(arrived_ref, got_ref, own_ref, ext_ref, mine_ref, wide, wide_refs):
    core = lax.axis_index("core")
    mine = pl.multiple_of(core * 2 * LAGS, 2 * LAGS)
    for g in range(CHIPS):
        for slot in range(2):
            at = (2 * g + slot) * (LAGS + PAD)
            wide[core, at : at + LAGS, :] = arrived_ref[g, pl.ds(mine + slot * LAGS, LAGS), :].astype(F32)
            wide[1 - core, at : at + LAGS, :] = got_ref[g, slot * LAGS : (slot + 1) * LAGS, :].astype(F32)
    total = LAGS * LANES
    lane = iota((4 * CHIPS, LANES), 1)
    for b in range(LAGS):
        halves = [wide[c, pl.ds(b, 2 * CHIPS, stride=LAGS + PAD), :].reshape(CHIPS // 4, 1, 8, LANES) for c in range(2)]
        plane = jnp.concatenate(halves, axis=1).reshape(4 * CHIPS, LANES)
        ext_ref[:, b * LANES : (b + 1) * LANES] = plane.astype(BF16)
        moved = jnp.where(
            lane < LANES - LAGS, pltpu.roll(plane, LANES - LAGS, 1), pltpu.roll(plane, LANES - LAGS - 1, 1)
        )
        moved = jnp.where(lane == LANES - 1, 0.0, moved)
        ext_ref[:, total + b * LANES : total + (b + 1) * LANES] = moved.astype(BF16)

    def write(row, lane, piece):
        mine_ref[row : row + CHIPS, lane : lane + LANES] = piece

    lay_out_refs(own_ref, wide_refs, write)


def correlate_kernel(ext_ref, mine_ref, other_ref, out_hbm, wide, refs, sums, sem):
    total = LAGS * LANES
    core = lax.axis_index("core")
    half = NREF // 2

    def write(row, lane, piece):
        row = pl.multiple_of((1 - core) * half + row, CHIPS)
        refs[pl.ds(row, CHIPS), lane : lane + LANES] = piece

    refs[pl.ds(pl.multiple_of(core * half, half), half), :] = mine_ref[...]
    lay_out_refs(other_ref, wide, write)
    rows = ext_ref.shape[0]
    copies = []
    lag = 1
    for step, per in enumerate(LAG_STEPS):
        windows = [ext_ref[:, pl.ds((lag + i) * LANES, total)] for i in range(per)]
        part = dot_nt(jnp.concatenate(windows, axis=0), refs[...]) * (1.0 / math.sqrt(total))
        for i in range(per):
            sums[:, (lag - 1 + i) * NREF : (lag + i) * NREF] = part[i * rows : (i + 1) * rows]
        span = pl.ds((lag - 1) * NREF, per * NREF)
        copies.append(pltpu.make_async_copy(sums.at[:, span], out_hbm.at[0, :, span], sem.at[step]))
        copies[-1].start()
        lag += per
    for copy in copies:
        copy.wait()


def swap_cores(x):
    return lax.ppermute(x, "core", [(0, 1), (1, 0)])


def on_device(raw, taps, row_channel, ref_channel, owner_of_row):
    rows_dev, samples = raw.shape
    total = samples // STRIDE
    window = BLOCK * STRIDE + 2 * HALO
    half = jax.ShapeDtypeStruct((CHIPS, 2 * LAGS, LANES), BF16)
    plain = jax.ShapeDtypeStruct((NREF // 2, total), BF16)
    ids = row_channel.reshape(-1, LANES)
    dec = pl.pallas_call(
        decimate_kernel,
        out_shape=jax.ShapeDtypeStruct((rows_dev, total), BF16),
        in_specs=[HBM, VMEM],
        out_specs=VMEM,
        scratch_shapes=[
            pltpu.VMEM((rows_dev, samples + 2 * HALO), BF16),
            pltpu.VMEM((8, 3 * LANES), F32),
            pltpu.VMEM((BLOCK, window), BF16),
            pltpu.VMEM((rows_dev, total), BF16),
            pltpu.SemaphoreType.DMA,
        ],
        compiler_params=params(52),
        name="decimate",
    )(raw, taps.reshape(1, TAPS))
    got = swap_cores(dec)
    select, keep = pl.pallas_call(
        find_kernel,
        out_shape=(jax.ShapeDtypeStruct((NREF // 2, rows_dev), BF16), plain),
        in_specs=[VMEM] * 3,
        out_specs=(VMEM, VMEM),
        compiler_params=params(),
        name="find",
    )(ids, ref_channel.reshape(1, NREF), dec)
    packet_shape = jax.ShapeDtypeStruct((CHIPS, 6 * LAGS, LANES), BF16)
    packet = pl.pallas_call(
        route_kernel,
        out_shape=packet_shape,
        in_specs=[VMEM, VMEM],
        out_specs=VMEM,
        scratch_shapes=[pltpu.VMEM((CHIPS * (4 * LAGS + PAD), LANES), F32)],
        compiler_params=params(),
        cost_estimate=pl.CostEstimate(flops=100_000_000, bytes_accessed=4_000_000, transcendentals=0),
        name="route",
    )(dec, owner_of_row.reshape(1, rows_dev))
    packet = pl.pallas_call(
        add_refs_kernel,
        out_shape=packet_shape,
        in_specs=[VMEM] * 4,
        out_specs=VMEM,
        scratch_shapes=[pltpu.VMEM((CHIPS * (2 * LAGS + PAD), LANES), F32)],
        input_output_aliases={0: 0},
        compiler_params=params(),
        name="add_refs",
    )(packet, select, keep, got)
    arrived = lax.all_to_all(packet, SAME, 0, 0, tiled=True)
    spread, rows_give = pl.pallas_call(
        spread_kernel,
        out_shape=(half, half),
        in_specs=[VMEM],
        out_specs=(VMEM, VMEM),
        compiler_params=params(),
        name="spread",
    )(arrived)
    refs_own = lax.all_to_all(spread, SAME, 0, 0, tiled=True)
    rows_got = swap_cores(rows_give)
    ext, refs_mine = pl.pallas_call(
        widen_kernel,
        out_shape=(jax.ShapeDtypeStruct((4 * CHIPS, 2 * total), BF16), plain),
        in_specs=[VMEM, VMEM, VMEM],
        out_specs=(VMEM, VMEM),
        scratch_shapes=[
            pltpu.VMEM((2, CHIPS * 2 * (LAGS + PAD), LANES), F32),
            pltpu.VMEM((CHIPS * (2 * LAGS + PAD), LANES), F32),
        ],
        compiler_params=params(),
        name="widen",
    )(arrived, rows_got, refs_own)
    refs_other = swap_cores(refs_own)
    return pl.pallas_call(
        correlate_kernel,
        out_shape=jax.ShapeDtypeStruct((1, 4 * CHIPS, LAGS * NREF), F32),
        in_specs=[VMEM, VMEM, VMEM],
        out_specs=HBM,
        scratch_shapes=[
            pltpu.VMEM((CHIPS * (2 * LAGS + PAD), LANES), F32),
            pltpu.VMEM((NREF, total), BF16),
            pltpu.VMEM((4 * CHIPS, LAGS * NREF), F32),
            pltpu.SemaphoreType.DMA((len(LAG_STEPS),)),
        ],
        compiler_params=params(24),
        name="correlate",
    )(ext, refs_mine, refs_other)


def solution(mesh):
    parts = Mesh(mesh.devices.reshape(4, 4, 2, 4), AXES)
    return jax.shard_map(
        on_device,
        mesh=parts,
        in_specs=(P(AXES, None), P(), P(), P(), P(AXES, None)),
        out_specs=P(AXES, None, None),
        check_vma=False,
    )
```
